256 devices in a mesh: dp: 16 (over z_hi, x), sp: 16 (over y, z_lo, core).
Axes of the slice: x: 4, y: 4, z: 8 (z_hi: 4, z_lo: 2; z = z_hi * 2 + z_lo), core: 2. Of those that a mesh axis runs over, the one named last changes fastest.
Arguments:
- features: bfloat16 [16, 32, 128, 640], P('dp', 'sp'), may hold values from -20 to 20
- timestep: int32 [16], P('dp'), may hold values from 0 to 999
- group_gain: float32 [640], replicated, may hold values from 0.5 to 1.5
- conv_weight: bfloat16 [3, 3, 640, 640], replicated, may hold values from -0.078125 to 0.078125
- time_weight: bfloat16 [320, 640], replicated, may hold values from -0.3125 to 0.3125
- norm_gain: float32 [640], replicated, may hold values from 0.5 to 1.5
- qkv_weight: bfloat16 [640, 1920], replicated, may hold values from -6 to 6
- out_weight: bfloat16 [640, 640], replicated, may hold values from -0.25 to 0.25
- cotangent: bfloat16 [16, 32, 128, 640], P('dp', 'sp'), may hold values from -1 to 1
Outputs:
- updated: bfloat16 [16, 32, 128, 640], P('dp', 'sp')
- out_grad: float32 [640, 640], replicated
The draws below stay inside these ranges and needn't reach their ends.
All inputs are finite; a program needn't handle non-finite values.
Results may differ from the reference program's by a relative error of at most 0.02.
Values may be sent and summed in bfloat16 or wider, within the bound.
A program may use at most 128 MiB of HBM per device.

```python
import math
import jax
import jax.numpy as jnp
from jax import lax

C = 640
HEADS = 16
GROUPS = 32
TEMB = 320
WIDTH = 128
HEAD_DIM = 40
SAMPLES = 16
HEIGHT = 32
SEQ = 4096


def draw_features(key, part):
    key = jax.random.fold_in(key, 11)
    base_key, scale_key = jax.random.split(key)
    full_shape = (SAMPLES, HEIGHT, WIDTH, C)
    position = jnp.arange(HEIGHT, dtype=jnp.float32) / max(HEIGHT - 1, 1)
    channel_scale = 10.0 ** jax.random.uniform(scale_key, (C,), minval=-0.5, maxval=0.5)
    raw_values = jnp.clip(jax.random.normal(base_key, full_shape), -5.0, 5.0)
    row_scale = 3.0 ** position
    return (0.3 * raw_values * row_scale[None, :, None, None] * channel_scale).astype(jnp.bfloat16)


def draw_qkv_weight(key, part):
    key = jax.random.fold_in(key, 23)
    full_shape = (C, HEADS, 3, C // HEADS)
    column_scale = jnp.array([2.0, 2.0, 1.0], jnp.float32)[None, None, :, None] / math.sqrt(C)
    raw_values = jnp.clip(jax.random.normal(key, full_shape), -4.0, 4.0) * column_scale
    return raw_values.reshape(C, 3 * C).astype(jnp.bfloat16)


def draw_cotangent(key, part):
    key = jax.random.fold_in(key, 37)
    noise_key, sign_key = jax.random.split(key)
    full_shape = (SAMPLES, HEIGHT, WIDTH, C)
    noise_scale = 1.0 / math.sqrt(SAMPLES * HEIGHT * WIDTH)
    offset = 8.0 / (WIDTH * math.sqrt(SAMPLES * HEIGHT))
    signs = jax.random.randint(sign_key, (SAMPLES, HEIGHT, 1, C), 0, 2).astype(jnp.float32) * 2.0 - 1.0
    noise = jnp.clip(jax.random.normal(noise_key, full_shape), -5.0, 5.0) * noise_scale
    return (signs * offset + noise).astype(jnp.bfloat16)


def touch_ends(drawn, stream_key, low, largest):
    longest = drawn.shape.index(max(drawn.shape))
    spots = []
    for shift in (0, 1):
        where = [jax.random.randint(jax.random.fold_in(stream_key, axis), (), 0, length) for axis, length in enumerate(drawn.shape)]
        where[longest] = (where[longest] + shift) % drawn.shape[longest]
        spots.append(tuple(where))
    return drawn.at[spots[0]].set(low).at[spots[1]].set(largest)


def normal_values(stream_key, extent, scale, limit, held_as=jnp.bfloat16):
    return jnp.clip(scale * jax.random.normal(stream_key, extent, jnp.float32), -limit, limit).astype(held_as)


def setup_inputs(seed: int = 0) -> dict:
    seeds = jax.random.split(jax.random.key(seed), 10)
    features = draw_features(jax.random.fold_in(seeds[9], 71), 0)
    timestep = touch_ends(jax.random.randint(seeds[1], (SAMPLES,), 0, 1000), jax.random.fold_in(seeds[1], 1), 0, 999).astype(jnp.int32)
    group_gain = jnp.clip(1.0 + 0.1 * jax.random.normal(seeds[2], (C,), jnp.float32), 0.5, 1.5)
    conv_weight = normal_values(seeds[3], (3, 3, C, C), (9 * C) ** -0.5, 0.078125)
    time_weight = normal_values(seeds[4], (TEMB, C), TEMB ** -0.5, 0.3125)
    norm_gain = jnp.clip(1.0 + 0.1 * jax.random.normal(seeds[5], (C,), jnp.float32), 0.5, 1.5)
    qkv_weight = draw_qkv_weight(jax.random.fold_in(seeds[9], 71), 0)
    out_weight = normal_values(seeds[7], (C, C), C ** -0.5, 0.25)
    cotangent = draw_cotangent(jax.random.fold_in(seeds[9], 71), 0)
    return dict(features=features, timestep=timestep, group_gain=group_gain, conv_weight=conv_weight, time_weight=time_weight, norm_gain=norm_gain, qkv_weight=qkv_weight, out_weight=out_weight, cotangent=cotangent)


def attend_block(queries, key_rows, value_rows, score_scale):
    scores = lax.dot_general(queries, key_rows, (((1,), (1,)), ((), ())), preferred_element_type=jnp.float32) * score_scale
    row_top = lax.optimization_barrier(jnp.max(scores, axis=-1, keepdims=True))
    weights = jnp.exp(scores - row_top)
    probabilities = (weights / lax.optimization_barrier(jnp.sum(weights, axis=-1, keepdims=True))).astype(jnp.bfloat16)
    return jnp.dot(probabilities, value_rows, preferred_element_type=jnp.float32)

def head_attention(triple, block_rows, score_scale):
    head_dim = triple.shape[-1]
    blocks = triple[0].reshape(-1, block_rows, head_dim)
    result = lax.map(lambda query_block: attend_block(query_block, triple[1], triple[2], score_scale), blocks)
    return result.reshape(-1, head_dim).astype(jnp.bfloat16)

def time_embed(timestep, time_weight):
    half_dim = time_weight.shape[0] // 2
    frequencies = jnp.exp(-math.log(10000.0) * jnp.arange(half_dim, dtype=jnp.float32) / half_dim)
    angles = timestep.astype(jnp.float32)[:, None] * frequencies[None, :]
    embedding = jnp.concatenate([jnp.cos(angles), jnp.sin(angles)], axis=-1)
    embed_act = jax.nn.silu(embedding).astype(jnp.bfloat16)
    return jnp.dot(embed_act, time_weight, preferred_element_type=jnp.float32)

def layer_norm(hidden, norm_gain):
    float_hidden = hidden.astype(jnp.float32)
    centred = float_hidden - lax.optimization_barrier(jnp.mean(float_hidden, axis=-1, keepdims=True))
    variance = lax.optimization_barrier(jnp.mean(centred * centred, axis=-1, keepdims=True))
    return (centred * lax.rsqrt(variance + 1e-05) * norm_gain).astype(jnp.bfloat16)

def reference(features, timestep, group_gain, conv_weight, time_weight, norm_gain, qkv_weight, out_weight, cotangent):
    per_group = C // GROUPS
    float_feats = features.astype(jnp.float32).reshape(SAMPLES, SEQ, GROUPS, per_group)
    cell_count = SEQ * per_group
    group_mean = lax.optimization_barrier(jnp.sum(float_feats, axis=(1, 3))) / cell_count
    group_var = lax.optimization_barrier(jnp.sum(float_feats * float_feats, axis=(1, 3))) / cell_count - group_mean * group_mean
    scaled = (float_feats - group_mean[:, None, :, None]) * lax.rsqrt(group_var + 1e-05)[:, None, :, None]
    activated = jax.nn.silu(scaled.reshape(SAMPLES, HEIGHT, WIDTH, C) * group_gain).astype(jnp.bfloat16)
    padded = jnp.pad(activated, ((0, 0), (1, 1), (1, 1), (0, 0)))
    conv_sum = jnp.zeros((SAMPLES * SEQ, C), jnp.float32)
    for row_off in range(3):
        for col_off in range(3):
            window = padded[:, row_off:row_off + HEIGHT, col_off:col_off + WIDTH].reshape(-1, C)
            conv_sum = conv_sum + jnp.dot(window, conv_weight[row_off, col_off], preferred_element_type=jnp.float32)
    time_bias = time_embed(timestep, time_weight)
    hidden = (features.astype(jnp.float32).reshape(SAMPLES, SEQ, C) + conv_sum.reshape(SAMPLES, SEQ, C) + time_bias[:, None, :]).astype(jnp.bfloat16)
    normed = layer_norm(hidden, norm_gain)
    projected = jnp.dot(normed.reshape(-1, C), qkv_weight, preferred_element_type=jnp.float32).astype(jnp.bfloat16)
    triples = projected.reshape(SAMPLES, SEQ, HEADS, 3, HEAD_DIM).transpose(0, 2, 3, 1, 4).reshape(SAMPLES * HEADS, 3, SEQ, HEAD_DIM)
    block_rows = math.gcd(SEQ, 512)
    score_scale = 1.0 / math.sqrt(HEAD_DIM)
    per_head = lax.map(lambda triple: head_attention(triple, block_rows, score_scale), triples)
    attended = per_head.reshape(SAMPLES, HEADS, SEQ, HEAD_DIM).transpose(0, 2, 1, 3).reshape(SAMPLES * SEQ, C)
    mixed_out = jnp.dot(attended, out_weight, preferred_element_type=jnp.float32)
    updated = (hidden.reshape(-1, C).astype(jnp.float32) + mixed_out).astype(jnp.bfloat16).reshape(SAMPLES, HEIGHT, WIDTH, C)
    out_grad = lax.dot_general(attended, cotangent.reshape(-1, C), (((0,), (0,)), ((), ())), preferred_element_type=jnp.float32)
    return (updated, out_grad)
```

```python
import functools
import math

import jax
import jax.numpy as jnp
from jax import lax
from jax.experimental import pallas as pl
from jax.experimental.pallas import tpu as pltpu
from jax.sharding import PartitionSpec as P

HEADS = 16
GROUPS = 32
C = 640
HD = 40
W = 128
TEMB = 320
ROWS = 2
T = ROWS * W
L = 128
HP = 48
NSP = 16
NDP = 16
f32 = jnp.float32
bf16 = jnp.bfloat16
NT = (((1,), (1,)), ((), ()))
TN = (((0,), (0,)), ((), ()))
CK = 512
NC = NSP * T // CK


def split3(v):
    hi = v.astype(bf16).astype(f32)
    rest = v - hi
    mid = rest.astype(bf16).astype(f32)
    return hi, mid, rest - mid


def stack_rows(rows, width):
    r = lax.broadcasted_iota(jnp.int32, (16, width), 0)
    out = jnp.zeros((16, width), f32)
    for i, v in enumerate(rows):
        out = jnp.where(r == i, v, out)
    return out.astype(bf16)


def kernel(
    ts_ref, ggain_ref, ngain_ref, feat_hbm, convw_hbm, timew_hbm, qkvw_hbm, outw_hbm, cot_hbm,
    upd_ref, grad_ref,
    fext, convw, timew, qkvw, outw, cot, wq, wo, cols, hid, stat, xsend, x, s_buf, m_buf,
    at_send, at, g_send, g, rs_send, rs, fin,
    local_sem, stat_ss, stat_rs, halo_ss, halo_rs, x_ss, x_rs, at_ss, at_rs, g_ss, g_rs,
    rs_ss, rs_rs, ag_ss, ag_rs, fin_ss, fin_rs, core_ss,
):
    me = lax.axis_index("sp")
    dp = lax.axis_index("dp")

    def sp_peer(t):
        return lax.rem(me + t, NSP)

    def dp_peer(t):
        return lax.rem(dp + t, NDP)

    def to_sp(src, dst, ss, rs_, j):
        return pltpu.make_async_remote_copy(
            src_ref=src, dst_ref=dst, send_sem=ss, recv_sem=rs_, device_id={"sp": j},
            device_id_type=pl.DeviceIdType.MESH)

    def to_dp(src, dst, ss, rs_, j):
        return pltpu.make_async_remote_copy(
            src_ref=src, dst_ref=dst, send_sem=ss, recv_sem=rs_, device_id={"dp": j},
            device_id_type=pl.DeviceIdType.MESH)

    def loop(lo, hi, body):
        def step(i, c):
            body(i)
            return c
        lax.fori_loop(lo, hi, step, 0)

    barrier = pltpu.get_barrier_semaphore()

    def greet(t):
        pl.semaphore_signal(barrier, inc=1, device_id={"sp": sp_peer(t)},
                            device_id_type=pl.DeviceIdType.MESH)
        pl.semaphore_signal(barrier, inc=1, device_id={"dp": dp_peer(t)},
                            device_id_type=pl.DeviceIdType.MESH)
    loop(1, NSP, greet)

    def fetch(i, src, dst):
        c = pltpu.make_async_copy(src, dst, local_sem.at[i])
        c.start()
        return c
    get_feat = fetch(0, feat_hbm, fext.at[W:W + T])
    get_timew = fetch(1, timew_hbm, timew)
    get_qkvw = fetch(2, qkvw_hbm, qkvw)
    get_convw = fetch(3, convw_hbm, convw)
    get_outw = fetch(4, outw_hbm, outw)
    get_cot = fetch(5, cot_hbm, cot)

    chan = lax.broadcasted_iota(jnp.int32, (C, L), 0)
    grp = lax.broadcasted_iota(jnp.int32, (C, L), 1)
    per_group = C // GROUPS
    member = ((chan >= grp * per_group) & (chan < grp * per_group + per_group))
    member = member.astype(f32).astype(bf16)
    get_feat.wait()
    feats = fext[W:W + T].astype(f32)
    s1 = jnp.sum(feats, axis=0, keepdims=True)
    s2 = jnp.sum(feats * feats, axis=0, keepdims=True)
    parts = jnp.dot(stack_rows(split3(s1) + split3(s2), C), member, preferred_element_type=f32)
    r8 = lax.broadcasted_iota(jnp.int32, (8, L), 0)
    t1 = parts[0:1] + parts[1:2] + parts[2:3]
    t2 = parts[3:4] + parts[4:5] + parts[5:6]
    stat[me] = jnp.where(r8 == 0, t1, jnp.where(r8 == 1, t2, 0.0))

    pl.semaphore_wait(barrier, NSP - 1 + NDP - 1)

    loop(1, NSP, lambda t: to_sp(
        stat.at[me], stat.at[me], stat_ss.at[sp_peer(t)], stat_rs.at[me], sp_peer(t)).start())
    up = to_sp(fext.at[W:2 * W], fext.at[3 * W:4 * W], halo_ss.at[0], halo_rs.at[0],
               lax.max(me - 1, 0))
    down = to_sp(fext.at[2 * W:3 * W], fext.at[0:W], halo_ss.at[1], halo_rs.at[1],
                 lax.min(me + 1, NSP - 1))

    @pl.when(me > 0)
    def _():
        up.start()

    @pl.when(me < NSP - 1)
    def _():
        down.start()

    get_timew.wait()
    half = TEMB // 2
    ti = lax.broadcasted_iota(jnp.int32, (8, TEMB), 1)
    tf = jnp.where(ti < half, ti, ti - half).astype(f32)
    freq = jnp.exp(-math.log(10000.0) * tf / half)
    angle = ts_ref[0].astype(f32) * freq
    emb = jnp.where(ti < half, jnp.cos(angle), jnp.sin(angle))
    emb = emb / (1.0 + jnp.exp(-emb))
    time_bias = jnp.dot(emb.astype(bf16), timew[...], preferred_element_type=f32)[0:1]

    get_qkvw.wait()
    lane = lax.broadcasted_iota(jnp.int32, (1, L), 1)
    for j in range(HEADS):
        base = (3 * HD * j) // L * L
        off = 3 * HD * j - base
        if off == 0:
            piece = qkvw[:, base:base + L].astype(f32)
        elif base + 2 * L <= 3 * C:
            piece = pltpu.roll(qkvw[:, base:base + 2 * L].astype(f32), 2 * L - off, axis=1)[:, :L]
        else:
            piece = pltpu.roll(qkvw[:, base:base + L].astype(f32), L - off, axis=1)
        piece = jnp.where(lane < 3 * HD, piece, 0.0).astype(bf16)
        wq[j // 2, :, (j % 2) * L:(j % 2) * L + L] = piece
    get_outw.wait()
    for j in range(HEADS):
        if (HD * j) % 16 == 0:
            rows = outw[HD * j:HD * j + HP] if j < HEADS - 1 else outw[HD * j:HD * j + HD]
            rows = rows.astype(f32)[:HD]
        else:
            rows = outw[HD * j - 8:HD * j + HD].astype(f32)[8:]
        wo[HP * j:HP * j + HP] = jnp.concatenate(
            [rows, jnp.zeros((HP - HD, C), f32)], axis=0).astype(bf16)
    at[me] = jnp.zeros((HP, T), bf16)

    loop(1, NSP, lambda t: to_sp(
        stat.at[sp_peer(t)], stat.at[sp_peer(t)], stat_ss.at[sp_peer(t)],
        stat_rs.at[sp_peer(t)], sp_peer(t)).wait_recv())
    total = jnp.sum(stat[...], axis=0)
    cells = float(NSP * T * per_group)
    mean = total[0:1] / cells
    rstd = lax.rsqrt(total[1:2] / cells - mean * mean + 1e-5)
    chan_t = lax.broadcasted_iota(jnp.int32, (L, C), 1)
    grp_t = lax.broadcasted_iota(jnp.int32, (L, C), 0)
    member_t = ((chan_t >= grp_t * per_group) & (chan_t < grp_t * per_group + per_group))
    member_t = member_t.astype(f32).astype(bf16)
    wide = jnp.dot(stack_rows(split3(mean) + split3(rstd), L), member_t,
                   preferred_element_type=f32)
    mean_c = wide[0:1] + wide[1:2] + wide[2:3]
    rstd_c = wide[3:4] + wide[4:5] + wide[5:6]
    col = lax.broadcasted_iota(jnp.int32, (W, C), 0)

    def activate(r, keep):
        v = (fext[r * W:(r + 1) * W].astype(f32) - mean_c) * rstd_c * ggain_ref[...]
        a = v / (1.0 + jnp.exp(-v))
        if keep is not None:
            a = jnp.where(keep, a, 0.0)
        here = slice(r * W, (r + 1) * W)
        cols[here, 0:C] = jnp.where(col == 0, 0.0, pltpu.roll(a, 1, axis=0)).astype(bf16)
        cols[here, C:2 * C] = a.astype(bf16)
        cols[here, 2 * C:3 * C] = jnp.where(
            col == W - 1, 0.0, pltpu.roll(a, W - 1, axis=0)).astype(bf16)

    activate(1, None)
    activate(2, None)

    @pl.when(me > 0)
    def _():
        down.wait_recv()

    @pl.when(me == 0)
    def _():
        fext[0:W] = jnp.zeros((W, C), bf16)

    @pl.when(me < NSP - 1)
    def _():
        up.wait_recv()

    @pl.when(me == NSP - 1)
    def _():
        fext[3 * W:4 * W] = jnp.zeros((W, C), bf16)

    activate(0, me > 0)
    activate(3, me < NSP - 1)

    get_convw.wait()
    conv = fext[W:W + T].astype(f32) + time_bias
    for a in range(3):
        conv = conv + jnp.dot(cols[a * W:a * W + T], convw[a], preferred_element_type=f32)
    hidden = conv.astype(bf16)
    hid[...] = hidden
    h = hidden.astype(f32)
    centred = h - jnp.mean(h, axis=1, keepdims=True)
    variance = jnp.mean(centred * centred, axis=1, keepdims=True)
    normed = (centred * lax.rsqrt(variance + 1e-5) * ngain_ref[...]).astype(bf16)

    scale = jnp.where(lane < HD, math.log2(math.e) / math.sqrt(HD), 1.0)
    ones = jnp.where(lane >= 3 * HD, 1.0, 0.0)

    def send_x(j):
        return to_sp(xsend.at[j], x.at[me], x_ss.at[j], x_rs.at[me], j)

    def project(u):
        chip = lax.rem(me // 2 + u, NSP // 2)
        pair = jnp.dot(normed, wq[chip], preferred_element_type=f32)
        for k in range(2):
            xsend[2 * chip + k] = (pair[:, k * L:(k + 1) * L] * scale + ones).astype(bf16)
        for k in range(2):
            @pl.when(2 * chip + k != me)
            def _():
                send_x(2 * chip + k).start()
    loop(0, NSP // 2, project)
    x[me] = xsend[me]

    def recv_x(t):
        j = sp_peer(t)
        to_sp(x.at[j], x.at[j], x_ss.at[j], x_rs.at[j], j).wait_recv()
    loop(1, NSP, recv_x)
    get_cot.wait()

    def query(j):
        q = pltpu.roll(x[j].astype(f32), HD, axis=1)
        return jnp.where((lane >= HD) & (lane < 2 * HD), q, 0.0).astype(bf16)

    def keys(c):
        per = CK // T
        return x[c * per:(c + 1) * per].reshape(CK, L)

    def scores(q, buf, c, top):
        s = lax.dot_general(q, keys(c), NT, preferred_element_type=f32)
        s_buf[buf, :, c * CK:(c + 1) * CK] = s
        for i in range(CK // L):
            top = jnp.maximum(top, s[:, i * L:(i + 1) * L])
        return top

    def weigh(m, buf, c, z):
        p = jnp.exp2(s_buf[buf, :, c * CK:(c + 1) * CK] - m).astype(bf16)
        return z + jnp.dot(p, keys(c), preferred_element_type=f32)

    lowest = jnp.full((T, L), -jnp.inf, f32)
    hrow = lax.broadcasted_iota(jnp.int32, (HP, T), 0)

    def attend(t, cur, nxt):
        m = jnp.max(m_buf[...], axis=1, keepdims=True)
        q = query(sp_peer(t + 2))
        top = lowest
        z = jnp.zeros((T, L), f32)
        for c in range(NC):
            top = scores(q, nxt, c, top)
            z = weigh(m, cur, c, z)
        m_buf[...] = top
        zt = (z / z[:, 3 * HD:3 * HD + 1]).T[2 * HD:]
        return jnp.where(hrow < HD, zt, 0.0).astype(bf16)

    def send_at(j):
        return to_sp(at_send.at[j], at.at[me], at_ss.at[j], at_rs.at[me], j)

    def recv_at(j):
        return to_sp(at.at[j], at.at[j], at_ss.at[j], at_rs.at[j], j)

    def send_g(j):
        return to_sp(g_send.at[j], g.at[me], g_ss.at[j], g_rs.at[me], j)

    def source(t):
        return lax.rem(me + 2 * NSP - 1 - t, NSP)

    top = lowest
    q0 = query(sp_peer(1))
    for c in range(NC):
        top = scores(q0, 0, c, top)
    m_buf[...] = top

    def two_steps(u):
        t = 2 * u
        first = lax.select(u >= 2, source(t - 4), me)
        second = lax.select(u >= 2, source(t - 3), me)

        @pl.when(u >= 2)
        def _():
            recv_at(first).wait_recv()
            recv_at(second).wait_recv()

        block = jnp.concatenate([at[first], at[second]], axis=0)
        both = jnp.dot(block, cot[...], preferred_element_type=f32).astype(bf16)
        g_send[first] = both[:HP]
        g_send[second] = both[HP:]
        at_send[sp_peer(t + 1)] = attend(t, 0, 1)
        send_at(sp_peer(t + 1)).start()

        @pl.when(u >= 2)
        def _():
            send_g(first).start()
            send_g(second).start()

        at_send[sp_peer(t + 2)] = attend(t + 1, 1, 0)

        @pl.when(u < NSP // 2 - 1)
        def _():
            send_at(sp_peer(t + 2)).start()
    loop(0, NSP // 2, two_steps)

    at[me] = at_send[me]
    last = [source(t) for t in range(12, 15)]
    for j in last:
        recv_at(j).wait_recv()
    block = jnp.concatenate([at[j] for j in last] + [at[me]], axis=0)
    final = jnp.dot(block, cot[...], preferred_element_type=f32).astype(bf16)
    for i, j in enumerate(last):
        g_send[j] = final[i * HP:(i + 1) * HP]
        send_g(j).start()
    g[me] = final[3 * HP:]

    mixed = lax.dot_general(at[...].reshape(NSP * HP, T), wo[...], TN, preferred_element_type=f32)
    upd_ref[...] = (hid[...].astype(f32) + mixed).astype(bf16)

    def recv_g(t):
        j = sp_peer(t)
        to_sp(g.at[j], g.at[j], g_ss.at[j], g_rs.at[j], j).wait_recv()
    loop(1, NSP, recv_g)
    here = jnp.zeros((HP, C), f32)
    for j in range(NSP):
        here = here + g[j].astype(f32)
    here = here.astype(bf16)
    for i in range(15):
        rs_send[i] = here[16 * (i // 5):16 * (i // 5) + 16, L * (i % 5):L * (i % 5) + L]
    rs_send[15] = jnp.zeros((16, L), bf16)

    def send_rs(t):
        j = dp_peer(t)
        return to_dp(rs_send.at[j], rs.at[dp], rs_ss.at[j], rs_rs.at[dp], j)
    loop(1, NDP, lambda t: send_rs(t).start())
    rs[dp] = rs_send[dp]

    def recv_rs(t):
        j = dp_peer(t)
        to_dp(rs.at[j], rs.at[j], rs_ss.at[j], rs_rs.at[j], j).wait_recv()
    loop(1, NDP, recv_rs)
    fin[me, dp] = jnp.sum(rs[...].astype(f32), axis=0).astype(bf16)

    def send_ag(t):
        j = dp_peer(t)
        return to_dp(fin.at[me, dp], fin.at[me, dp], ag_ss.at[j], ag_rs.at[dp], j)
    loop(1, NDP, lambda t: send_ag(t).start())

    def recv_ag(t):
        j = dp_peer(t)
        to_dp(fin.at[me, j], fin.at[me, j], ag_ss.at[j], ag_rs.at[j], j).wait_recv()
    loop(1, NDP, recv_ag)

    sibling = me + 1 - 2 * lax.rem(me, 2)

    def send_fin(u):
        j = lax.rem(me + 2 * u, NSP)
        return to_sp(fin.at[me], fin.at[me], fin_ss.at[j], fin_rs.at[me], j)

    def pass_on(j):
        return to_sp(fin.at[j], fin.at[j], core_ss.at[j], fin_rs.at[j], sibling)
    loop(1, NSP // 2, lambda u: send_fin(u).start())
    pass_on(me).start()

    def relay(u):
        j = lax.rem(me + NSP - 2 * u, NSP)
        to_sp(fin.at[j], fin.at[j], fin_ss.at[j], fin_rs.at[j], j).wait_recv()
        pass_on(j).start()
    loop(1, NSP // 2, relay)

    def recv_core(u):
        j = lax.rem(sibling + NSP - 2 * u, NSP)
        to_sp(fin.at[j], fin.at[j], core_ss.at[j], fin_rs.at[j], sibling).wait_recv()
    loop(0, NSP // 2, recv_core)

    for j in range(HEADS):
        for i in range(15):
            a, b = i // 5, i % 5
            grad_ref[HP * j + 16 * a:HP * j + 16 * a + 16, L * b:L * b + L] = fin[j, i]

    @pl.when(me > 0)
    def _():
        up.wait_send()

    @pl.when(me < NSP - 1)
    def _():
        down.wait_send()

    def drain(t):
        j = sp_peer(t)
        to_sp(stat.at[me], stat.at[me], stat_ss.at[j], stat_rs.at[me], j).wait_send()
        send_x(j).wait_send()
        send_at(j).wait_send()
        send_g(j).wait_send()
        send_rs(t).wait_send()
        send_ag(t).wait_send()
    loop(1, NSP, drain)

    def drain_fin(u):
        send_fin(u).wait_send()
        pass_on(lax.rem(me + NSP - 2 * u, NSP)).wait_send()
    loop(1, NSP // 2, drain_fin)
    pass_on(me).wait_send()


def on_device(features, timestep, group_gain, conv_weight, time_weight, norm_gain, qkv_weight,
              out_weight, cotangent):
    vmem = pl.BlockSpec(memory_space=pltpu.VMEM)
    hbm = pl.BlockSpec(memory_space=pl.ANY)
    dma = pltpu.SemaphoreType.DMA
    updated, grad = pl.pallas_call(
        kernel,
        out_shape=(
            jax.ShapeDtypeStruct((T, C), bf16),
            jax.ShapeDtypeStruct((HEADS * HP, C), bf16),
        ),
        in_specs=[pl.BlockSpec(memory_space=pltpu.SMEM), vmem, vmem] + [hbm] * 6,
        out_specs=(vmem, vmem),
        scratch_shapes=[
            pltpu.VMEM((4 * W, C), bf16),
            pltpu.VMEM((3, 3 * C, C), bf16),
            pltpu.VMEM((TEMB, C), bf16),
            pltpu.VMEM((C, 3 * C), bf16),
            pltpu.VMEM((C, C), bf16),
            pltpu.VMEM((T, C), bf16),
            pltpu.VMEM((HEADS // 2, C, 2 * L), bf16),
            pltpu.VMEM((HEADS * HP, C), bf16),
            pltpu.VMEM((4 * W, 3 * C), bf16),
            pltpu.VMEM((T, C), bf16),
            pltpu.VMEM((NSP, 8, L), f32),
            pltpu.VMEM((NSP, T, L), bf16),
            pltpu.VMEM((NSP, T, L), bf16),
            pltpu.VMEM((2, T, NSP * T), f32),
            pltpu.VMEM((T, L), f32),
            pltpu.VMEM((NSP, HP, T), bf16),
            pltpu.VMEM((NSP, HP, T), bf16),
            pltpu.VMEM((NSP, HP, C), bf16),
            pltpu.VMEM((NSP, HP, C), bf16),
            pltpu.VMEM((NDP, 16, L), bf16),
            pltpu.VMEM((NDP, 16, L), bf16),
            pltpu.VMEM((NSP, NDP, 16, L), bf16),
            dma((6,)), dma((16,)), dma((16,)), dma((2,)), dma((2,)), dma((16,)), dma((16,)),
            dma((16,)), dma((16,)), dma((16,)), dma((16,)), dma((16,)), dma((16,)),
            dma((16,)), dma((16,)), dma((16,)), dma((16,)), dma((16,)),
        ],
        compiler_params=pltpu.CompilerParams(
            collective_id=0, has_side_effects=True, vmem_limit_bytes=60 * 2**20),
        name="level",
    )(
        timestep, group_gain.reshape(1, C), norm_gain.reshape(1, C), features.reshape(T, C),
        conv_weight.reshape(3, 3 * C, C), time_weight, qkv_weight, out_weight,
        cotangent.reshape(T, C),
    )
    out_grad = grad.reshape(HEADS, HP, C)[:, :HD].reshape(C, C).astype(f32)
    return updated.reshape(1, ROWS, W, C), out_grad


def solution(mesh):
    slab = P("dp", "sp", None, None)
    return jax.shard_map(
        on_device, mesh=mesh,
        in_specs=(slab, P("dp"), P(), P(), P(), P(), P(), P(), slab),
        out_specs=(slab, P()), check_vma=False,
    )
```

```python
import functools
import math

import jax
import jax.numpy as jnp
from jax import lax
from jax.experimental import pallas as pl
from jax.experimental.pallas import tpu as pltpu
from jax.sharding import PartitionSpec as P

HEADS = 16
GROUPS = 32
C = 640
HD = 40
W = 128
TEMB = 320
ROWS = 2
T = ROWS * W
L = 128
HP = 48
NSP = 16
NDP = 16
f32 = jnp.float32
bf16 = jnp.bfloat16
NT = (((1,), (1,)), ((), ()))
TN = (((0,), (0,)), ((), ()))
CK = 512


def split3(v):
    hi = v.astype(bf16).astype(f32)
    rest = v - hi
    mid = rest.astype(bf16).astype(f32)
    return hi, mid, rest - mid


def stack_rows(rows, width):
    r = lax.broadcasted_iota(jnp.int32, (16, width), 0)
    out = jnp.zeros((16, width), f32)
    for i, v in enumerate(rows):
        out = jnp.where(r == i, v, out)
    return out.astype(bf16)


def kernel(
    ts_ref, ggain_ref, ngain_ref, feat_hbm, convw_hbm, timew_hbm, qkvw_hbm, outw_hbm, cot_hbm,
    upd_ref, grad_ref,
    fext, convw, timew, qkvw, outw, cot, wq, wo, cols, hid, stat, xsend, x, s_buf, m_buf,
    at_send, at, g_send, g, part, other, rs_send, rs, zs, fin, z_own, m_own,
    local_sem, stat_ss, stat_rs, halo_ss, halo_rs, x_ss, x_rs, at_ss, at_rs, g_ss, g_rs,
    cot_ss, cot_rs, part_ss, part_rs, rs_ss, rs_rs, zs_ss, zs_rs, ag_ss, ag_rs, fin_ss, fin_rs, rest_ss, rest_rs, core_ss, core_rs,
):
    me = lax.axis_index("sp")
    dp = lax.axis_index("dp")

    def sp_peer(t):
        return lax.rem(me + t, NSP)

    y, z, core = me // 4, lax.rem(me // 2, 2), lax.rem(me, 2)
    zh, xi = dp // 4, lax.rem(dp, 4)

    chip = me // 2

    def x_peer(t):
        return zh * 4 + lax.rem(xi + t, 4)

    def zh_peer(t):
        return lax.rem(zh + t, 4) * 4 + xi

    def slab(dy, dz, dc):
        return lax.rem(y + dy, 4) * 4 + lax.rem(z + dz, 2) * 2 + lax.rem(core + dc, 2)

    def to_sp(src, dst, ss, rs_, j):
        return pltpu.make_async_remote_copy(
            src_ref=src, dst_ref=dst, send_sem=ss, recv_sem=rs_, device_id={"sp": j},
            device_id_type=pl.DeviceIdType.MESH)

    def to_dp(src, dst, ss, rs_, j):
        return pltpu.make_async_remote_copy(
            src_ref=src, dst_ref=dst, send_sem=ss, recv_sem=rs_, device_id={"dp": j},
            device_id_type=pl.DeviceIdType.MESH)

    def loop(lo, hi, body):
        def step(i, c):
            body(i)
            return c
        lax.fori_loop(lo, hi, step, 0)

    barrier = pltpu.get_barrier_semaphore()

    def greet(t):
        pl.semaphore_signal(barrier, inc=1, device_id={"sp": sp_peer(t)},
                            device_id_type=pl.DeviceIdType.MESH)

    for t in range(1, 4):
        for j in (zh_peer(t), x_peer(t)):
            pl.semaphore_signal(barrier, inc=1, device_id={"dp": j},
                                device_id_type=pl.DeviceIdType.MESH)
    loop(1, NSP, greet)

    def fetch(i, src, dst):
        c = pltpu.make_async_copy(src, dst, local_sem.at[i])
        c.start()
        return c
    get_feat = fetch(0, feat_hbm, fext.at[W:W + T])

    chan = lax.broadcasted_iota(jnp.int32, (C, L), 0)
    grp = lax.broadcasted_iota(jnp.int32, (C, L), 1)
    per_group = C // GROUPS
    member = ((chan >= grp * per_group) & (chan < grp * per_group + per_group))
    member = member.astype(f32).astype(bf16)
    get_feat.wait()
    get_timew = fetch(1, timew_hbm, timew)
    get_qkvw = fetch(2, qkvw_hbm, qkvw)
    get_outw = fetch(4, outw_hbm, outw)
    get_convw = fetch(3, convw_hbm, convw)
    get_cot = fetch(5, cot_hbm, cot.at[core])
    feats = fext[W:W + T].astype(f32)
    s1 = jnp.sum(feats, axis=0, keepdims=True)
    s2 = jnp.sum(feats * feats, axis=0, keepdims=True)
    parts = jnp.dot(stack_rows(split3(s1) + split3(s2), C), member, preferred_element_type=f32)
    r8 = lax.broadcasted_iota(jnp.int32, (8, L), 0)
    t1 = parts[0:1] + parts[1:2] + parts[2:3]
    t2 = parts[3:4] + parts[4:5] + parts[5:6]
    stat[me] = jnp.where(r8 == 0, t1, jnp.where(r8 == 1, t2, 0.0))

    pl.semaphore_wait(barrier, NSP - 1 + 3 + 3)

    loop(1, NSP, lambda t: to_sp(
        stat.at[me], stat.at[me], stat_ss.at[sp_peer(t)], stat_rs.at[me], sp_peer(t)).start())
    up = to_sp(fext.at[W:2 * W], fext.at[3 * W:4 * W], halo_ss.at[0], halo_rs.at[0],
               lax.max(me - 1, 0))
    down = to_sp(fext.at[2 * W:3 * W], fext.at[0:W], halo_ss.at[1], halo_rs.at[1],
                 lax.min(me + 1, NSP - 1))

    @pl.when(me > 0)
    def _():
        up.start()

    @pl.when(me < NSP - 1)
    def _():
        down.start()

    sibling = slab(0, 0, 1)
    swap_cot = to_sp(cot.at[core], cot.at[core], cot_ss.at[0], cot_rs.at[0], sibling)

    get_timew.wait()
    half = TEMB // 2
    ti = lax.broadcasted_iota(jnp.int32, (8, TEMB), 1)
    tf = jnp.where(ti < half, ti, ti - half).astype(f32)
    freq = jnp.exp(-math.log(10000.0) * tf / half)
    angle = ts_ref[...].astype(f32).reshape(1, 1) * freq
    emb = jnp.where(ti < half, jnp.cos(angle), jnp.sin(angle))
    emb = emb / (1.0 + jnp.exp(-emb))
    time_bias = jnp.dot(emb.astype(bf16), timew[...], preferred_element_type=f32)[0:1]

    get_qkvw.wait()
    lane = lax.broadcasted_iota(jnp.int32, (1, L), 1)
    for j in range(HEADS):
        base = (3 * HD * j) // L * L
        off = 3 * HD * j - base
        if off == 0:
            piece = qkvw[:, base:base + L].astype(f32)
        elif base + 2 * L <= 3 * C:
            piece = pltpu.roll(qkvw[:, base:base + 2 * L].astype(f32), 2 * L - off, axis=1)[:, :L]
        else:
            piece = pltpu.roll(qkvw[:, base:base + L].astype(f32), L - off, axis=1)
        piece = jnp.where(lane < 3 * HD, piece, 0.0).astype(bf16)
        wq[j // 2, :, (j % 2) * L:(j % 2) * L + L] = piece
    get_outw.wait()
    for j in range(HEADS):
        if (HD * j) % 16 == 0:
            rows = outw[HD * j:HD * j + HP] if j < HEADS - 1 else outw[HD * j:HD * j + HD]
            rows = rows.astype(f32)[:HD]
        else:
            rows = outw[HD * j - 8:HD * j + HD].astype(f32)[8:]
        here = slice(HP * (j // 2), HP * (j // 2) + HP)
        wo[j % 2, here] = jnp.concatenate(
            [rows, jnp.zeros((HP - HD, C), f32)], axis=0).astype(bf16)
    at[chip] = jnp.zeros((HP, 2 * T), bf16)

    loop(1, NSP, lambda t: to_sp(
        stat.at[sp_peer(t)], stat.at[sp_peer(t)], stat_ss.at[sp_peer(t)],
        stat_rs.at[sp_peer(t)], sp_peer(t)).wait_recv())
    total = jnp.sum(stat[...], axis=0)
    cells = float(NSP * T * per_group)
    mean = total[0:1] / cells
    rstd = lax.rsqrt(total[1:2] / cells - mean * mean + 1e-5)
    chan_t = lax.broadcasted_iota(jnp.int32, (L, C), 1)
    grp_t = lax.broadcasted_iota(jnp.int32, (L, C), 0)
    member_t = ((chan_t >= grp_t * per_group) & (chan_t < grp_t * per_group + per_group))
    member_t = member_t.astype(f32).astype(bf16)
    wide = jnp.dot(stack_rows(split3(mean) + split3(rstd), L), member_t,
                   preferred_element_type=f32)
    mean_c = wide[0:1] + wide[1:2] + wide[2:3]
    rstd_c = wide[3:4] + wide[4:5] + wide[5:6]
    col = lax.broadcasted_iota(jnp.int32, (W, C), 0)

    def activate(r, keep):
        v = (fext[r * W:(r + 1) * W].astype(f32) - mean_c) * rstd_c * ggain_ref[...].reshape(1, C)
        a = v / (1.0 + jnp.exp(-v))
        if keep is not None:
            a = jnp.where(keep, a, 0.0)
        here = slice(r * W, (r + 1) * W)
        cols[here, 0:C] = jnp.where(col == 0, 0.0, pltpu.roll(a, 1, axis=0)).astype(bf16)
        cols[here, C:2 * C] = a.astype(bf16)
        cols[here, 2 * C:3 * C] = jnp.where(
            col == W - 1, 0.0, pltpu.roll(a, W - 1, axis=0)).astype(bf16)

    activate(1, None)
    activate(2, None)

    @pl.when(me > 0)
    def _():
        down.wait_recv()

    @pl.when(me == 0)
    def _():
        fext[0:W] = jnp.zeros((W, C), bf16)

    @pl.when(me < NSP - 1)
    def _():
        up.wait_recv()

    @pl.when(me == NSP - 1)
    def _():
        fext[3 * W:4 * W] = jnp.zeros((W, C), bf16)

    activate(0, me > 0)
    activate(3, me < NSP - 1)

    get_convw.wait()
    get_cot.wait()
    swap_cot.start()
    conv = fext[W:W + T].astype(f32) + time_bias
    for a in range(3):
        conv = conv + jnp.dot(cols[a * W:a * W + T], convw[a], preferred_element_type=f32)
    hidden = conv.astype(bf16)
    hid[...] = hidden
    h = hidden.astype(f32)
    centred = h - jnp.mean(h, axis=1, keepdims=True)
    variance = jnp.mean(centred * centred, axis=1, keepdims=True)
    normed = (centred * lax.rsqrt(variance + 1e-5) * ngain_ref[...].reshape(1, C)).astype(bf16)

    scale = jnp.where(lane < HD, math.log2(math.e) / math.sqrt(HD), 1.0)
    ones = jnp.where(lane >= 3 * HD, 1.0, 0.0)

    def send_x(j):
        return to_sp(xsend.at[j], x.at[me], x_ss.at[j], x_rs.at[me], j)

    for dy, dz in ((0, 1), (1, 0), (3, 0), (2, 0), (0, 0), (1, 1), (3, 1), (2, 1)):
        there = slab(dy, dz, 0) // 2
        pair = jnp.dot(normed, wq[there], preferred_element_type=f32)
        for k in range(2):
            xsend[2 * there + k] = (pair[:, k * L:(k + 1) * L] * scale + ones).astype(bf16)
        if dy == 0 and dz == 0:
            send_x(slab(0, 0, 1)).start()
            x[me] = xsend[me]
        else:
            for k in range(2):
                send_x(2 * there + k).start()

    def recv_x(j):
        to_sp(x.at[j], x.at[j], x_ss.at[j], x_rs.at[j], j).wait_recv()
    for dy in range(4):
        for dc in range(2):
            if dy or dc:
                recv_x(slab(dy, 0, dc))

    def query(j):
        q = pltpu.roll(x[j].astype(f32), HD, axis=1)
        return jnp.where((lane >= HD) & (lane < 2 * HD), q, 0.0).astype(bf16)

    def keys(kind, c):
        first = {"all": 2 * c, "own": 4 * c + 2 * z, "other": 4 * c + 2 * (1 - z)}[kind]
        return x[pl.ds(first, 2)].reshape(2 * T, L)

    chunks = {"all": NSP // 2, "own": NSP // 4, "other": NSP // 4}

    def scores(q, kind, buf, c, top):
        s = lax.dot_general(q, keys(kind, c), NT, preferred_element_type=f32)
        s_buf[buf, :, c * CK:(c + 1) * CK] = s
        for i in range(CK // L):
            top = jnp.maximum(top, s[:, i * L:(i + 1) * L])
        return top

    def weigh(m, kind, buf, c, acc):
        p = jnp.exp2(s_buf[buf, :, c * CK:(c + 1) * CK] - m).astype(bf16)
        return acc + jnp.dot(p, keys(kind, c), preferred_element_type=f32)

    lowest = jnp.full((T, L), -jnp.inf, f32)
    hrow = lax.broadcasted_iota(jnp.int32, (HP, T), 0)

    def begin(q, kind):
        top = lowest
        for c in range(chunks[kind]):
            top = scores(q, kind, 0, c, top)
        m_buf[...] = top

    def attend(kind, buf, nxt, before=None):
        m = jnp.max(m_buf[...], axis=1, keepdims=True)
        if before is None:
            acc = jnp.zeros((T, L), f32)
        else:
            m0 = m_own[before][:, :1]
            m = jnp.maximum(m, m0)
            acc = z_own[before] * jnp.exp2(m0 - m)
        top = lowest
        for c in range(NSP // 2):
            if nxt is not None and c < chunks[nxt[1]]:
                top = scores(nxt[0], nxt[1], 1 - buf, c, top)
            if c < chunks[kind]:
                acc = weigh(m, kind, buf, c, acc)
        if nxt is not None:
            m_buf[...] = top
        return acc, m

    def finish(acc):
        at_t = (acc / acc[:, 3 * HD:3 * HD + 1]).T[2 * HD:]
        return jnp.where(hrow < HD, at_t, 0.0).astype(bf16)

    def dy_of(p):
        k = lax.rem(p, 4)
        return lax.select(k == 0, 2, lax.select(k == 1, 1, lax.select(k == 2, 3, 0)))

    def target(p):
        return slab(dy_of(p), 1 - p // 4, 0) // 2

    def source(p):
        return slab(4 - dy_of(p), 1 - p // 4, 0) // 2

    def send_at(c):
        return to_sp(at_send.at[c], at.at[chip], at_ss.at[c], at_rs.at[chip], 2 * c + core)

    def recv_at(c):
        return to_sp(at.at[c], at.at[c], at_ss.at[c], at_rs.at[c], 2 * c + core)

    def send_g(c):
        return to_sp(g_send.at[c], g.at[chip], g_ss.at[c], g_rs.at[chip], 2 * c + core)

    def i32(v):
        return jnp.int32(v)

    begin(query(2 * target(i32(4))), "own")

    def own_pair(u):
        now, later = target(4 + u), target(4 + lax.rem(u + 1, 4))
        for k in range(2):
            acc, m = attend("own", k, (query(2 * now + 1 if k == 0 else 2 * later), "own"))
            z_own[2 * u + k] = acc
            m_own[2 * u + k] = jnp.broadcast_to(m, (T, L))
    loop(0, 4, own_pair)

    for dy in range(4):
        for dc in range(2):
            recv_x(slab(dy, 1, dc))
    swap_cot.wait_recv()
    cots = cot.reshape(2 * T, C)

    def grads(p, live):
        c = lax.select(live, source(p), chip)

        @pl.when(live)
        def _():
            recv_at(c).wait_recv()

        g_send[c] = jnp.dot(at[c], cots[...], preferred_element_type=f32).astype(bf16)

        def start():
            @pl.when(live)
            def _():
                send_g(c).start()
        return start

    begin(query(2 * target(i32(0))), "all")

    def cross_pair(u, last):
        start = grads(lax.max(u - 2, 0), u >= 2)
        now, later = target(u), target(u + 1)
        acc, _ = attend("all", 0, (query(2 * now + 1), "all"))
        at_send[now, :, 0:T] = finish(acc)
        start()
        acc, _ = attend("all", 1, (query(2 * later), "other" if last else "all"))
        at_send[now, :, T:2 * T] = finish(acc)
        send_at(now).start()
    loop(0, 3, lambda u: cross_pair(u, False))
    cross_pair(i32(3), True)

    def side_pair(u, last):
        start = grads(lax.select(u == 0, 2, u + 1), u != 1)
        now, later = target(4 + u), target(4 + lax.rem(u + 1, 4))
        acc, _ = attend("other", 0, (query(2 * now + 1), "other"), before=2 * u)
        at_send[now, :, 0:T] = finish(acc)
        start()
        acc, _ = attend("other", 1, None if last else (query(2 * later), "other"),
                        before=2 * u + 1)
        at_send[now, :, T:2 * T] = finish(acc)
        if not last:
            send_at(now).start()
    loop(0, 3, lambda u: side_pair(u, False))
    side_pair(i32(3), True)

    at[chip] = at_send[chip]
    last = [source(i32(p)) for p in (5, 6)]
    for c in last:
        recv_at(c).wait_recv()
    block = jnp.concatenate([at[c] for c in last] + [at[chip]], axis=0)
    final = jnp.dot(block, cots[...], preferred_element_type=f32).astype(bf16)
    for i, c in enumerate(last):
        g_send[c] = final[i * HP:(i + 1) * HP]
        send_g(c).start()
    g[chip] = final[2 * HP:]

    mixed = lax.dot_general(at[...].reshape(NSP // 2 * HP, 2 * T), wo[core], TN,
                            preferred_element_type=f32)
    part[0] = mixed[:T]
    part[1] = mixed[T:]
    swap_part = to_sp(part.at[1 - core], other, part_ss.at[0], part_rs.at[0], sibling)
    swap_part.start()

    def recv_g(c):
        to_sp(g.at[c], g.at[c], g_ss.at[c], g_rs.at[c], 2 * c + core).wait_recv()
    loop(1, NSP // 2, lambda t: recv_g(lax.rem(chip + t, NSP // 2)))
    here = jnp.zeros((HP, C), f32)
    for j in range(NSP // 2):
        here = here + g[j].astype(f32)
    here = here.astype(bf16)
    for i in range(16):
        tile = jnp.zeros((16, L), bf16)
        if i < 15:
            tile = here[16 * (i // 5):16 * (i // 5) + 16, L * (i % 5):L * (i % 5) + L]
        rs_send[i // 4, 16 * (i % 4):16 * (i % 4) + 16] = tile

    def send_rs(t):
        k = lax.rem(xi + t, 4)
        return to_dp(rs_send.at[k], rs.at[xi], rs_ss.at[t], rs_rs.at[xi], x_peer(t))

    def send_zs(t):
        return to_dp(zs.at[zh], zs.at[zh], zs_ss.at[t], zs_rs.at[zh], zh_peer(t))
    for t in (2, 1, 3):
        send_rs(t).start()
    rs[xi] = rs_send[xi]
    for t in (1, 3, 2):
        k = lax.rem(xi + t, 4)
        to_dp(rs.at[k], rs.at[k], rs_ss.at[t], rs_rs.at[k], x_peer(t)).wait_recv()
    zs[zh] = jnp.sum(rs[...].astype(f32), axis=0).astype(bf16)
    for t in (2, 1, 3):
        send_zs(t).start()
    for t in (1, 3, 2):
        k = lax.rem(zh + t, 4)
        to_dp(zs.at[k], zs.at[k], zs_ss.at[t], zs_rs.at[k], zh_peer(t)).wait_recv()
    fin[me, 0] = jnp.sum(zs[...].astype(f32), axis=0).astype(bf16)

    def send_ag(t):
        return to_dp(fin.at[me, 0], fin.at[me, 4 - t], ag_ss.at[t], ag_rs.at[4 - t], x_peer(t))

    def send_own(u):
        j = lax.rem(me + 2 * u, NSP)
        return to_sp(fin.at[me, 0], fin.at[me, 0], fin_ss.at[j], fin_rs.at[me], j)

    def send_rest(u):
        j = lax.rem(me + 2 * u, NSP)
        return to_sp(fin.at[me, pl.ds(1, 3)], fin.at[me, pl.ds(1, 3)], rest_ss.at[j],
                     rest_rs.at[me], j)
    def pass_on(j):
        return to_sp(fin.at[j], fin.at[j], core_ss.at[j], core_rs.at[j], sibling)
    for t in (2, 1, 3):
        send_ag(t).start()
    loop(1, NSP // 2, lambda u: send_own(u).start())
    swap_part.wait_recv()
    upd_ref[...] = (hid[...].astype(f32) + part[core] + other[...]).astype(bf16)

    for k in (1, 3, 2):
        to_dp(fin.at[me, k], fin.at[me, k], ag_ss.at[k], ag_rs.at[k], x_peer(k)).wait_recv()
    loop(1, NSP // 2, lambda u: send_rest(u).start())
    pass_on(me).start()

    def relay(u):
        j = lax.rem(me + NSP - 2 * u, NSP)
        to_sp(fin.at[j, 0], fin.at[j, 0], fin_ss.at[j], fin_rs.at[j], j).wait_recv()
        to_sp(fin.at[j, pl.ds(1, 3)], fin.at[j, pl.ds(1, 3)], rest_ss.at[j], rest_rs.at[j],
              j).wait_recv()
        pass_on(j).start()
    loop(1, NSP // 2, relay)

    def recv_core(u):
        j = lax.rem(sibling + NSP - 2 * u, NSP)
        to_sp(fin.at[j], fin.at[j], core_ss.at[j], core_rs.at[j], sibling).wait_recv()
    loop(0, NSP // 2, recv_core)

    quarter = [lax.rem(k + 4 - xi, 4) for k in range(4)]

    def head_rows(j):
        tiles = [fin[j, quarter[i // 4], 16 * (i % 4):16 * (i % 4) + 16] for i in range(15)]
        return jnp.concatenate(
            [jnp.concatenate(tiles[5 * a:5 * a + 5], axis=1) for a in range(3)], axis=0)
    for j in range(0, HEADS, 2):
        two = jnp.concatenate(
            [head_rows(j).astype(f32)[:HD], head_rows(j + 1).astype(f32)[:HD]], axis=0)
        grad_ref[HD * j:HD * j + 2 * HD] = two.astype(bf16)

    @pl.when(me > 0)
    def _():
        up.wait_send()

    @pl.when(me < NSP - 1)
    def _():
        down.wait_send()

    def drain(t):
        j = sp_peer(t)
        to_sp(stat.at[me], stat.at[me], stat_ss.at[j], stat_rs.at[me], j).wait_send()
        send_x(j).wait_send()
    loop(1, NSP, drain)

    def drain_pair(t):
        c = lax.rem(chip + t, NSP // 2)
        send_at(c).wait_send()
        send_g(c).wait_send()
    loop(1, NSP // 2, drain_pair)
    swap_cot.wait_send()
    swap_part.wait_send()
    for t in range(1, 4):
        send_rs(t).wait_send()
        send_zs(t).wait_send()
        send_ag(t).wait_send()

    def drain_fin(u):
        send_own(u).wait_send()
        send_rest(u).wait_send()
        pass_on(lax.rem(me + NSP - 2 * u, NSP)).wait_send()
    loop(1, NSP // 2, drain_fin)
    pass_on(me).wait_send()


def on_device(features, timestep, group_gain, conv_weight, time_weight, norm_gain, qkv_weight,
              out_weight, cotangent):
    vmem = pl.BlockSpec(memory_space=pltpu.VMEM)
    hbm = pl.BlockSpec(memory_space=pl.ANY)
    dma = pltpu.SemaphoreType.DMA
    updated, grad = pl.pallas_call(
        kernel,
        out_shape=(
            jax.ShapeDtypeStruct((T, C), bf16),
            jax.ShapeDtypeStruct((C, C), bf16),
        ),
        in_specs=[vmem, vmem, vmem] + [hbm] * 6,
        out_specs=(vmem, vmem),
        scratch_shapes=[
            pltpu.VMEM((4 * W, C), bf16),
            pltpu.VMEM((3, 3 * C, C), bf16),
            pltpu.VMEM((TEMB, C), bf16),
            pltpu.VMEM((C, 3 * C), bf16),
            pltpu.VMEM((C, C), bf16),
            pltpu.VMEM((2, T, C), bf16),
            pltpu.VMEM((HEADS // 2, C, 2 * L), bf16),
            pltpu.VMEM((2, HEADS // 2 * HP, C), bf16),
            pltpu.VMEM((4 * W, 3 * C), bf16),
            pltpu.VMEM((T, C), bf16),
            pltpu.VMEM((NSP, 8, L), f32),
            pltpu.VMEM((NSP, T, L), bf16),
            pltpu.VMEM((NSP, T, L), bf16),
            pltpu.VMEM((2, T, NSP * T), f32),
            pltpu.VMEM((T, L), f32),
            pltpu.VMEM((NSP // 2, HP, 2 * T), bf16),
            pltpu.VMEM((NSP // 2, HP, 2 * T), bf16),
            pltpu.VMEM((NSP // 2, HP, C), bf16),
            pltpu.VMEM((NSP // 2, HP, C), bf16),
            pltpu.VMEM((2, T, C), f32),
            pltpu.VMEM((T, C), f32),
            pltpu.VMEM((4, 64, L), bf16),
            pltpu.VMEM((4, 64, L), bf16),
            pltpu.VMEM((4, 64, L), bf16),
            pltpu.VMEM((NSP, 4, 64, L), bf16),
            pltpu.VMEM((8, T, L), f32),
            pltpu.VMEM((8, T, L), f32),
            dma((6,)), dma((16,)), dma((16,)), dma((2,)), dma((2,)), dma((16,)), dma((16,)),
            dma((8,)), dma((8,)), dma((8,)), dma((8,)),
            dma((1,)), dma((1,)), dma((1,)), dma((1,)),
            dma((4,)), dma((4,)), dma((4,)), dma((4,)), dma((4,)), dma((4,)),
            dma((16,)), dma((16,)), dma((16,)), dma((16,)), dma((16,)), dma((16,)),
        ],
        compiler_params=pltpu.CompilerParams(
            collective_id=0, has_side_effects=True, vmem_limit_bytes=60 * 2**20),
        name="level",
    )(
        timestep, group_gain, norm_gain, features.reshape(T, C),
        conv_weight.reshape(3, 3 * C, C), time_weight, qkv_weight, out_weight,
        cotangent.reshape(T, C),
    )
    return updated.reshape(1, ROWS, W, C), grad.astype(f32)


def solution(mesh):
    slab = P("dp", "sp", None, None)
    return jax.shard_map(
        on_device, mesh=mesh,
        in_specs=(slab, P("dp"), P(), P(), P(), P(), P(), P(), slab),
        out_specs=(slab, P()), check_vma=False,
    )
```

```python
import functools
import math

import jax
import jax.numpy as jnp
from jax import lax
from jax.experimental import pallas as pl
from jax.experimental.pallas import tpu as pltpu
from jax.sharding import PartitionSpec as P

HEADS = 16
GROUPS = 32
C = 640
HD = 40
W = 128
TEMB = 320
ROWS = 2
T = ROWS * W
L = 128
HP = 48
NSP = 16
NDP = 16
f32 = jnp.float32
bf16 = jnp.bfloat16
NT = (((1,), (1,)), ((), ()))
TN = (((0,), (0,)), ((), ()))
CK = 512


def split3(v):
    hi = v.astype(bf16).astype(f32)
    rest = v - hi
    mid = rest.astype(bf16).astype(f32)
    return hi, mid, rest - mid


def stack_rows(rows, width):
    r = lax.broadcasted_iota(jnp.int32, (16, width), 0)
    out = jnp.zeros((16, width), f32)
    for i, v in enumerate(rows):
        out = jnp.where(r == i, v, out)
    return out.astype(bf16)


def kernel(
    ts_ref, ggain_ref, ngain_ref, feat_hbm, convw_hbm, timew_hbm, qkvw_hbm, outw_hbm, cot_hbm,
    upd_ref, fin_out,
    fext, convw, timew, qkvw, outw, cot, wq, wo, cols, hid, stat, xsend, x, s_buf, m_buf,
    at_send, at, g_send, g, part, other, zs, fin, z_own, m_own,
    local_sem, stat_ss, stat_rs, halo_ss, halo_rs, x_ss, x_rs, at_ss, at_rs, g_ss, g_rs,
    cot_ss, cot_rs, part_ss, part_rs, zs_ss, zs_rs, ag_ss, ag_rs, fin_ss, fin_rs, rest_ss, rest_rs, core_ss, core_rs,
):
    me = lax.axis_index("sp")
    dp = lax.axis_index("dp")

    def sp_peer(t):
        return lax.rem(me + t, NSP)

    y, z, core = me // 4, lax.rem(me // 2, 2), lax.rem(me, 2)
    zh, xi = dp // 4, lax.rem(dp, 4)

    chip = me // 2

    def x_peer(t):
        return zh * 4 + lax.rem(xi + t, 4)

    def zh_peer(t):
        return lax.rem(zh + t, 4) * 4 + xi

    def slab(dy, dz, dc):
        return lax.rem(y + dy, 4) * 4 + lax.rem(z + dz, 2) * 2 + lax.rem(core + dc, 2)

    def to_sp(src, dst, ss, rs_, j):
        return pltpu.make_async_remote_copy(
            src_ref=src, dst_ref=dst, send_sem=ss, recv_sem=rs_, device_id={"sp": j},
            device_id_type=pl.DeviceIdType.MESH)

    def to_dp(src, dst, ss, rs_, j):
        return pltpu.make_async_remote_copy(
            src_ref=src, dst_ref=dst, send_sem=ss, recv_sem=rs_, device_id={"dp": j},
            device_id_type=pl.DeviceIdType.MESH)

    def loop(lo, hi, body):
        def step(i, c):
            body(i)
            return c
        lax.fori_loop(lo, hi, step, 0)

    barrier = pltpu.get_barrier_semaphore()

    def greet(t):
        pl.semaphore_signal(barrier, inc=1, device_id={"sp": sp_peer(t)},
                            device_id_type=pl.DeviceIdType.MESH)

    for t in range(1, 4):
        pl.semaphore_signal(barrier, inc=1, device_id={"dp": zh_peer(t)},
                            device_id_type=pl.DeviceIdType.MESH)
    for t in range(1, 4):
        for c in range(NSP // 2):
            pl.semaphore_signal(barrier, inc=1, device_id={"dp": x_peer(t), "sp": 2 * c + core},
                                device_id_type=pl.DeviceIdType.MESH)
    loop(1, NSP, greet)

    def fetch(i, src, dst):
        c = pltpu.make_async_copy(src, dst, local_sem.at[i])
        c.start()
        return c
    get_feat = fetch(0, feat_hbm, fext.at[W:W + T])

    chan = lax.broadcasted_iota(jnp.int32, (C, L), 0)
    grp = lax.broadcasted_iota(jnp.int32, (C, L), 1)
    per_group = C // GROUPS
    member = ((chan >= grp * per_group) & (chan < grp * per_group + per_group))
    member = member.astype(f32).astype(bf16)
    get_feat.wait()
    get_timew = fetch(1, timew_hbm, timew)
    get_qkvw = fetch(2, qkvw_hbm, qkvw)
    get_outw = fetch(4, outw_hbm, outw)
    get_convw = fetch(3, convw_hbm, convw)
    get_cot = fetch(5, cot_hbm, cot.at[core])
    feats = fext[W:W + T].astype(f32)
    s1 = jnp.sum(feats, axis=0, keepdims=True)
    s2 = jnp.sum(feats * feats, axis=0, keepdims=True)
    parts = jnp.dot(stack_rows(split3(s1) + split3(s2), C), member, preferred_element_type=f32)
    r8 = lax.broadcasted_iota(jnp.int32, (8, L), 0)
    t1 = parts[0:1] + parts[1:2] + parts[2:3]
    t2 = parts[3:4] + parts[4:5] + parts[5:6]
    stat[me] = jnp.where(r8 == 0, t1, jnp.where(r8 == 1, t2, 0.0))

    pl.semaphore_wait(barrier, NSP - 1 + 3 + 3 * NSP // 2)

    loop(1, NSP, lambda t: to_sp(
        stat.at[me], stat.at[me], stat_ss.at[sp_peer(t)], stat_rs.at[me], sp_peer(t)).start())
    up = to_sp(fext.at[W:2 * W], fext.at[3 * W:4 * W], halo_ss.at[0], halo_rs.at[0],
               lax.max(me - 1, 0))
    down = to_sp(fext.at[2 * W:3 * W], fext.at[0:W], halo_ss.at[1], halo_rs.at[1],
                 lax.min(me + 1, NSP - 1))

    @pl.when(me > 0)
    def _():
        up.start()

    @pl.when(me < NSP - 1)
    def _():
        down.start()

    sibling = slab(0, 0, 1)
    swap_cot = to_sp(cot.at[core], cot.at[core], cot_ss.at[0], cot_rs.at[0], sibling)

    get_timew.wait()
    half = TEMB // 2
    ti = lax.broadcasted_iota(jnp.int32, (8, TEMB), 1)
    tf = jnp.where(ti < half, ti, ti - half).astype(f32)
    freq = jnp.exp(-math.log(10000.0) * tf / half)
    angle = ts_ref[...].astype(f32).reshape(1, 1) * freq
    emb = jnp.where(ti < half, jnp.cos(angle), jnp.sin(angle))
    emb = emb / (1.0 + jnp.exp(-emb))
    time_bias = jnp.dot(emb.astype(bf16), timew[...], preferred_element_type=f32)[0:1]

    get_qkvw.wait()
    lane = lax.broadcasted_iota(jnp.int32, (1, L), 1)

    def regroup(r):
        here = pl.ds(pl.multiple_of(r * L, L), L)
        for j in range(HEADS):
            base = (3 * HD * j) // L * L
            off = 3 * HD * j - base
            width = 2 * L if 0 < off and base + 2 * L <= 3 * C else L
            piece = qkvw[here, base:base + width].astype(f32)
            if off:
                piece = pltpu.roll(piece, width - off, axis=1)[:, :L]
            piece = jnp.where(lane < 3 * HD, piece, 0.0).astype(bf16)
            wq[j // 2, here, (j % 2) * L:(j % 2) * L + L] = piece
    loop(0, C // L, regroup)
    get_outw.wait()
    for j in range(HEADS):
        if (HD * j) % 16 == 0:
            rows = outw[HD * j:HD * j + HP] if j < HEADS - 1 else outw[HD * j:HD * j + HD]
            rows = rows.astype(f32)[:HD]
        else:
            rows = outw[HD * j - 8:HD * j + HD].astype(f32)[8:]
        here = slice(HP * (j // 2), HP * (j // 2) + HP)
        wo[j % 2, here] = jnp.concatenate(
            [rows, jnp.zeros((HP - HD, C), f32)], axis=0).astype(bf16)
    at[chip] = jnp.zeros((HP, 2 * T), bf16)
    g_send[...] = jnp.zeros(g_send.shape, bf16)

    loop(1, NSP, lambda t: to_sp(
        stat.at[sp_peer(t)], stat.at[sp_peer(t)], stat_ss.at[sp_peer(t)],
        stat_rs.at[sp_peer(t)], sp_peer(t)).wait_recv())
    total = jnp.sum(stat[...], axis=0)
    cells = float(NSP * T * per_group)
    mean = total[0:1] / cells
    rstd = lax.rsqrt(total[1:2] / cells - mean * mean + 1e-5)
    chan_t = lax.broadcasted_iota(jnp.int32, (L, C), 1)
    grp_t = lax.broadcasted_iota(jnp.int32, (L, C), 0)
    member_t = ((chan_t >= grp_t * per_group) & (chan_t < grp_t * per_group + per_group))
    member_t = member_t.astype(f32).astype(bf16)
    wide = jnp.dot(stack_rows(split3(mean) + split3(rstd), L), member_t,
                   preferred_element_type=f32)
    mean_c = wide[0:1] + wide[1:2] + wide[2:3]
    rstd_c = wide[3:4] + wide[4:5] + wide[5:6]
    col = lax.broadcasted_iota(jnp.int32, (W, C), 0)

    def activate(r, keep):
        here = pl.ds(pl.multiple_of(r * W, W), W)
        v = (fext[here].astype(f32) - mean_c) * rstd_c * ggain_ref[...].reshape(1, C)
        a = v / (1.0 + jnp.exp(-v))
        a = jnp.where(keep, a, 0.0)
        cols[here, 0:C] = jnp.where(col == 0, 0.0, pltpu.roll(a, 1, axis=0)).astype(bf16)
        cols[here, C:2 * C] = a.astype(bf16)
        cols[here, 2 * C:3 * C] = jnp.where(
            col == W - 1, 0.0, pltpu.roll(a, W - 1, axis=0)).astype(bf16)

    loop(1, 3, lambda r: activate(r, r > 0))

    @pl.when(me > 0)
    def _():
        down.wait_recv()

    @pl.when(me == 0)
    def _():
        fext[0:W] = jnp.zeros((W, C), bf16)

    @pl.when(me < NSP - 1)
    def _():
        up.wait_recv()

    @pl.when(me == NSP - 1)
    def _():
        fext[3 * W:4 * W] = jnp.zeros((W, C), bf16)

    loop(0, 2, lambda r: activate(3 * r, jnp.where(r == 0, me > 0, me < NSP - 1)))

    get_convw.wait()
    get_cot.wait()
    swap_cot.start()
    conv = fext[W:W + T].astype(f32) + time_bias
    for a in range(3):
        conv = conv + jnp.dot(cols[a * W:a * W + T], convw[a], preferred_element_type=f32)
    hidden = conv.astype(bf16)
    hid[...] = hidden
    h = hidden.astype(f32)
    centred = h - jnp.mean(h, axis=1, keepdims=True)
    variance = jnp.mean(centred * centred, axis=1, keepdims=True)
    normed = (centred * lax.rsqrt(variance + 1e-5) * ngain_ref[...].reshape(1, C)).astype(bf16)

    scale = jnp.where(lane < HD, math.log2(math.e) / math.sqrt(HD), 1.0)
    ones = jnp.where(lane >= 3 * HD, 1.0, 0.0)

    def send_x(j):
        return to_sp(xsend.at[j], x.at[me], x_ss.at[j], x_rs.at[me], j)

    for dy, dz in ((0, 1), (1, 0), (3, 0), (2, 0), (0, 0), (1, 1), (3, 1), (2, 1)):
        there = slab(dy, dz, 0) // 2
        pair = jnp.dot(normed, wq[there], preferred_element_type=f32)
        for k in range(2):
            xsend[2 * there + k] = (pair[:, k * L:(k + 1) * L] * scale + ones).astype(bf16)
        if dy == 0 and dz == 0:
            send_x(slab(0, 0, 1)).start()
            x[me] = xsend[me]
        else:
            for k in range(2):
                send_x(2 * there + k).start()

    def recv_x(j):
        to_sp(x.at[j], x.at[j], x_ss.at[j], x_rs.at[j], j).wait_recv()
    for dy in range(4):
        for dc in range(2):
            if dy or dc:
                recv_x(slab(dy, 0, dc))

    def query(j):
        q = pltpu.roll(x[j].astype(f32), HD, axis=1)
        return jnp.where((lane >= HD) & (lane < 2 * HD), q, 0.0).astype(bf16)

    def keys(kind, c):
        first = {"all": 2 * c, "own": 4 * c + 2 * z, "other": 4 * c + 2 * (1 - z)}[kind]
        return x[pl.ds(first, 2)].reshape(2 * T, L)

    chunks = {"all": NSP // 2, "own": NSP // 4, "other": NSP // 4}

    def scores(q, kind, buf, c, top):
        s = lax.dot_general(q, keys(kind, c), NT, preferred_element_type=f32)
        s_buf[buf, :, c * CK:(c + 1) * CK] = s
        for i in range(CK // L):
            top = jnp.maximum(top, s[:, i * L:(i + 1) * L])
        return top

    def weigh(m, kind, buf, c, acc):
        p = jnp.exp2(s_buf[buf, :, c * CK:(c + 1) * CK] - m).astype(bf16)
        return acc + jnp.dot(p, keys(kind, c), preferred_element_type=f32)

    lowest = jnp.full((T, L), -jnp.inf, f32)
    hrow = lax.broadcasted_iota(jnp.int32, (HP, T), 0)

    def begin(q, kind):
        top = lowest
        for c in range(chunks[kind]):
            top = scores(q, kind, 0, c, top)
        m_buf[...] = top

    def attend(kind, buf, nxt, before=None):
        m = jnp.max(m_buf[...], axis=1, keepdims=True)
        if before is None:
            acc = jnp.zeros((T, L), f32)
        else:
            m0 = m_own[before][:, :1]
            m = jnp.maximum(m, m0)
            acc = z_own[before] * jnp.exp2(m0 - m)
        top = lowest
        for c in range(NSP // 2):
            if nxt is not None and c < chunks[nxt[1]]:
                top = scores(nxt[0], nxt[1], 1 - buf, c, top)
            if c < chunks[kind]:
                acc = weigh(m, kind, buf, c, acc)
        if nxt is not None:
            m_buf[...] = top
        return acc, m

    def finish(acc):
        at_t = (acc / acc[:, 3 * HD:3 * HD + 1]).T[2 * HD:]
        return jnp.where(hrow < HD, at_t, 0.0).astype(bf16)

    def dy_of(p):
        k = lax.rem(p, 4)
        return lax.select(k == 0, 2, lax.select(k == 1, 1, lax.select(k == 2, 3, 0)))

    def target(p):
        return slab(dy_of(p), 1 - p // 4, 0) // 2

    def source(p):
        return slab(4 - dy_of(p), 1 - p // 4, 0) // 2

    def send_at(c):
        return to_sp(at_send.at[c], at.at[chip], at_ss.at[c], at_rs.at[chip], 2 * c + core)

    def recv_at(c):
        return to_sp(at.at[c], at.at[c], at_ss.at[c], at_rs.at[c], 2 * c + core)

    def send_g(c, k):
        return pltpu.make_async_remote_copy(
            src_ref=g_send.at[c, k], dst_ref=g.at[xi, chip], send_sem=g_ss.at[c, k],
            recv_sem=g_rs.at[xi, chip], device_id={"dp": zh * 4 + k, "sp": 2 * c + core},
            device_id_type=pl.DeviceIdType.MESH)

    def put_g(c, rows):
        for i in range(15):
            a, b = i // 5, i % 5
            g_send[c, i // 4, 16 * (i % 4):16 * (i % 4) + 16] = (
                rows[16 * a:16 * a + 16, L * b:L * b + L])

    def i32(v):
        return jnp.int32(v)

    begin(query(2 * target(i32(4))), "own")

    def own_pair(u):
        now, later = target(4 + u), target(4 + lax.rem(u + 1, 4))
        for k in range(2):
            acc, m = attend("own", k, (query(2 * now + 1 if k == 0 else 2 * later), "own"))
            z_own[2 * u + k] = acc
            m_own[2 * u + k] = jnp.broadcast_to(m, (T, L))
    loop(0, 4, own_pair)

    for dy in range(4):
        for dc in range(2):
            recv_x(slab(dy, 1, dc))
    swap_cot.wait_recv()
    cots = cot.reshape(2 * T, C)

    def grads(p, live):
        c = lax.select(live, source(p), chip)

        @pl.when(live)
        def _():
            recv_at(c).wait_recv()

        put_g(c, jnp.dot(at[c], cots[...], preferred_element_type=f32).astype(bf16))

        def start():
            @pl.when(live)
            def _():
                for k in range(4):
                    send_g(c, k).start()
        return start

    begin(query(2 * target(i32(0))), "all")

    def cross_pair(u, last):
        start = grads(i32(0), jnp.bool_(True)) if last else None
        now, later = target(u), target(u + 1)
        acc, _ = attend("all", 0, (query(2 * now + 1), "all"))
        at_send[now, :, 0:T] = finish(acc)
        acc, _ = attend("all", 1, (query(2 * later), "other" if last else "all"))
        at_send[now, :, T:2 * T] = finish(acc)
        send_at(now).start()
        if last:
            start()
    loop(0, 3, lambda u: cross_pair(u, False))
    cross_pair(i32(3), True)

    def side_pair(u, last):
        start = grads(lax.select(u == 3, 3, u + 1), u != 2)
        now, later = target(4 + u), target(4 + lax.rem(u + 1, 4))
        acc, _ = attend("other", 0, (query(2 * now + 1), "other"), before=2 * u)
        at_send[now, :, 0:T] = finish(acc)
        acc, _ = attend("other", 1, None if last else (query(2 * later), "other"),
                        before=2 * u + 1)
        at_send[now, :, T:2 * T] = finish(acc)
        if not last:
            send_at(now).start()
        start()
    loop(0, 3, lambda u: side_pair(u, False))
    side_pair(i32(3), True)

    at[chip] = at_send[chip]
    last = [source(i32(p)) for p in (4, 5, 6)]
    for c in last:
        recv_at(c).wait_recv()
    block = jnp.concatenate([at[c] for c in last] + [at[chip]], axis=0)
    final = jnp.dot(block, cots[...], preferred_element_type=f32).astype(bf16)
    for i, c in enumerate(last):
        put_g(c, final[i * HP:(i + 1) * HP])
        for k in range(4):
            send_g(c, k).start()
    put_g(chip, final[3 * HP:])
    for t in range(1, 4):
        send_g(chip, lax.rem(xi + t, 4)).start()
    g[xi, chip] = g_send[chip, xi]

    def recv_g(t):
        k, c = lax.rem(xi + t // 8, 4), lax.rem(chip + t, 8)
        pltpu.make_async_remote_copy(
            src_ref=g.at[k, c], dst_ref=g.at[k, c], send_sem=g_ss.at[c, k],
            recv_sem=g_rs.at[k, c], device_id={"dp": zh * 4 + k, "sp": 2 * c + core},
            device_id_type=pl.DeviceIdType.MESH).wait_recv()
    loop(1, 4 * NSP // 2, recv_g)

    def add_g(k, total):
        return total + jnp.sum(g[k].astype(f32), axis=0)

    def send_zs(t):
        return to_dp(zs.at[zh], zs.at[zh], zs_ss.at[t], zs_rs.at[zh], zh_peer(t))
    zs[zh] = lax.fori_loop(0, 4, add_g, jnp.zeros((64, L), f32)).astype(bf16)
    for t in (2, 1, 3):
        send_zs(t).start()

    mixed = lax.dot_general(at[...].reshape(NSP // 2 * HP, 2 * T), wo[core], TN,
                            preferred_element_type=f32)
    part[0] = mixed[:T]
    part[1] = mixed[T:]
    swap_part = to_sp(part.at[1 - core], other, part_ss.at[0], part_rs.at[0], sibling)
    swap_part.start()

    for t in (1, 3, 2):
        k = lax.rem(zh + t, 4)
        to_dp(zs.at[k], zs.at[k], zs_ss.at[t], zs_rs.at[k], zh_peer(t)).wait_recv()
    fin[me, 0] = jnp.sum(zs[...].astype(f32), axis=0).astype(bf16)

    def send_ag(t):
        return to_dp(fin.at[me, 0], fin.at[me, 4 - t], ag_ss.at[t], ag_rs.at[4 - t], x_peer(t))

    def send_own(u):
        j = lax.rem(me + 2 * u, NSP)
        return to_sp(fin.at[me, 0], fin.at[me, 0], fin_ss.at[j], fin_rs.at[me], j)

    def send_rest(u):
        j = lax.rem(me + 2 * u, NSP)
        return to_sp(fin.at[me, pl.ds(1, 3)], fin.at[me, pl.ds(1, 3)], rest_ss.at[j],
                     rest_rs.at[me], j)
    def pass_on(j):
        return to_sp(fin.at[j], fin.at[j], core_ss.at[j], core_rs.at[j], sibling)
    for t in (2, 1, 3):
        send_ag(t).start()
    loop(1, NSP // 2, lambda u: send_own(u).start())
    swap_part.wait_recv()
    upd_ref[...] = (hid[...].astype(f32) + part[core] + other[...]).astype(bf16)

    for k in (1, 3, 2):
        to_dp(fin.at[me, k], fin.at[me, k], ag_ss.at[k], ag_rs.at[k], x_peer(k)).wait_recv()
    loop(1, NSP // 2, lambda u: send_rest(u).start())
    pass_on(me).start()

    def relay(u):
        j = lax.rem(me + NSP - 2 * u, NSP)
        to_sp(fin.at[j, 0], fin.at[j, 0], fin_ss.at[j], fin_rs.at[j], j).wait_recv()
        to_sp(fin.at[j, pl.ds(1, 3)], fin.at[j, pl.ds(1, 3)], rest_ss.at[j], rest_rs.at[j],
              j).wait_recv()
        pass_on(j).start()
    loop(1, NSP // 2, relay)

    def recv_core(u):
        j = lax.rem(sibling + NSP - 2 * u, NSP)
        to_sp(fin.at[j], fin.at[j], core_ss.at[j], core_rs.at[j], sibling).wait_recv()
    loop(0, NSP // 2, recv_core)

    fin_out[...] = fin[...]

    @pl.when(me > 0)
    def _():
        up.wait_send()

    @pl.when(me < NSP - 1)
    def _():
        down.wait_send()

    def drain(t):
        j = sp_peer(t)
        to_sp(stat.at[me], stat.at[me], stat_ss.at[j], stat_rs.at[me], j).wait_send()
        send_x(j).wait_send()
    loop(1, NSP, drain)

    def drain_pair(t):
        c = lax.rem(chip + t, NSP // 2)
        send_at(c).wait_send()
        for k in range(4):
            send_g(c, k).wait_send()
    loop(1, NSP // 2, drain_pair)
    swap_cot.wait_send()
    swap_part.wait_send()
    for t in range(1, 4):
        send_g(chip, lax.rem(xi + t, 4)).wait_send()
        send_zs(t).wait_send()
        send_ag(t).wait_send()

    def drain_fin(u):
        send_own(u).wait_send()
        send_rest(u).wait_send()
        pass_on(lax.rem(me + NSP - 2 * u, NSP)).wait_send()
    loop(1, NSP // 2, drain_fin)
    pass_on(me).wait_send()


def outputs(fin_hbm, upd_hbm, upd_out, grad_out, fin, upd, grad, sem):
    xi = lax.rem(lax.axis_index("dp"), 4)
    take = pltpu.make_async_copy(upd_hbm, upd, sem.at[HEADS // 2])
    move = pltpu.make_async_copy(upd, upd_out, sem.at[HEADS // 2])

    def get(j):
        return pltpu.make_async_copy(fin_hbm.at[pl.ds(j, 2)], fin.at[pl.ds(j, 2)],
                                     sem.at[HEADS // 2 + 1 + j // 2])
    for j in range(0, HEADS, 2):
        get(j).start()
    take.start()
    quarter = [lax.rem(k + 4 - xi, 4) for k in range(4)]

    def head_rows(j):
        tiles = [fin[j, quarter[i // 4], 16 * (i % 4):16 * (i % 4) + 16] for i in range(15)]
        return jnp.concatenate(
            [jnp.concatenate(tiles[5 * a:5 * a + 5], axis=1) for a in range(3)], axis=0)
    for j in range(0, HEADS, 2):
        get(j).wait()
        two = jnp.concatenate(
            [head_rows(j).astype(f32)[:HD], head_rows(j + 1).astype(f32)[:HD]], axis=0)
        here = slice(HD * j, HD * j + 2 * HD)
        grad[here] = two
        pltpu.make_async_copy(grad.at[here], grad_out.at[here], sem.at[j // 2]).start()
    take.wait()
    move.start()
    for j in range(0, HEADS, 2):
        here = slice(HD * j, HD * j + 2 * HD)
        pltpu.make_async_copy(grad.at[here], grad_out.at[here], sem.at[j // 2]).wait()
    move.wait()


def on_device(features, timestep, group_gain, conv_weight, time_weight, norm_gain, qkv_weight,
              out_weight, cotangent):
    vmem = pl.BlockSpec(memory_space=pltpu.VMEM)
    hbm = pl.BlockSpec(memory_space=pl.ANY)
    dma = pltpu.SemaphoreType.DMA
    updated, tiles = pl.pallas_call(
        kernel,
        out_shape=(
            jax.ShapeDtypeStruct((T, C), bf16),
            jax.ShapeDtypeStruct((NSP, 4, 64, L), bf16),
        ),
        in_specs=[vmem, vmem, vmem] + [hbm] * 6,
        out_specs=(vmem, vmem),
        scratch_shapes=[
            pltpu.VMEM((4 * W, C), bf16),
            pltpu.VMEM((3, 3 * C, C), bf16),
            pltpu.VMEM((TEMB, C), bf16),
            pltpu.VMEM((C, 3 * C), bf16),
            pltpu.VMEM((C, C), bf16),
            pltpu.VMEM((2, T, C), bf16),
            pltpu.VMEM((HEADS // 2, C, 2 * L), bf16),
            pltpu.VMEM((2, HEADS // 2 * HP, C), bf16),
            pltpu.VMEM((4 * W, 3 * C), bf16),
            pltpu.VMEM((T, C), bf16),
            pltpu.VMEM((NSP, 8, L), f32),
            pltpu.VMEM((NSP, T, L), bf16),
            pltpu.VMEM((NSP, T, L), bf16),
            pltpu.VMEM((2, T, NSP * T), f32),
            pltpu.VMEM((T, L), f32),
            pltpu.VMEM((NSP // 2, HP, 2 * T), bf16),
            pltpu.VMEM((NSP // 2, HP, 2 * T), bf16),
            pltpu.VMEM((NSP // 2, 4, 64, L), bf16),
            pltpu.VMEM((4, NSP // 2, 64, L), bf16),
            pltpu.VMEM((2, T, C), f32),
            pltpu.VMEM((T, C), f32),
            pltpu.VMEM((4, 64, L), bf16),
            pltpu.VMEM((NSP, 4, 64, L), bf16),
            pltpu.VMEM((8, T, L), f32),
            pltpu.VMEM((8, T, L), f32),
            dma((6,)), dma((16,)), dma((16,)), dma((2,)), dma((2,)), dma((16,)), dma((16,)),
            dma((8,)), dma((8,)), dma((8, 4)), dma((4, 8)),
            dma((1,)), dma((1,)), dma((1,)), dma((1,)),
            dma((4,)), dma((4,)), dma((4,)), dma((4,)),
            dma((16,)), dma((16,)), dma((16,)), dma((16,)), dma((16,)), dma((16,)),
        ],
        compiler_params=pltpu.CompilerParams(
            collective_id=0, has_side_effects=True, vmem_limit_bytes=60 * 2**20),
        name="level",
    )(
        timestep, group_gain, norm_gain, features.reshape(T, C),
        conv_weight.reshape(3, 3 * C, C), time_weight, qkv_weight, out_weight,
        cotangent.reshape(T, C),
    )
    updated, out_grad = pl.pallas_call(
        outputs,
        out_shape=(
            jax.ShapeDtypeStruct((T, C), bf16),
            jax.ShapeDtypeStruct((C, C), f32),
        ),
        in_specs=[hbm, hbm],
        out_specs=(hbm, hbm),
        scratch_shapes=[
            pltpu.VMEM((NSP, 4, 64, L), bf16),
            pltpu.VMEM((T, C), bf16),
            pltpu.VMEM((C, C), f32),
            dma((HEADS + 1,)),
        ],
        compiler_params=pltpu.CompilerParams(vmem_limit_bytes=63 * 2**20),
        name="outputs",
    )(tiles, updated)
    return updated.reshape(1, ROWS, W, C), out_grad


def solution(mesh):
    slab = P("dp", "sp", None, None)
    return jax.shard_map(
        on_device, mesh=mesh,
        in_specs=(slab, P("dp"), P(), P(), P(), P(), P(), P(), slab),
        out_specs=(slab, P()), check_vma=False,
    )
```

```python
import functools
import math

import jax
import jax.numpy as jnp
from jax import lax
from jax.experimental import pallas as pl
from jax.experimental.pallas import tpu as pltpu
from jax.sharding import PartitionSpec as P

HEADS = 16
GROUPS = 32
C = 640
HD = 40
W = 128
TEMB = 320
ROWS = 2
T = ROWS * W
L = 128
HP = 48
NSP = 16
NDP = 16
f32 = jnp.float32
bf16 = jnp.bfloat16
NT = (((1,), (1,)), ((), ()))
TN = (((0,), (0,)), ((), ()))
CK = 512


def split3(v):
    hi = v.astype(bf16).astype(f32)
    rest = v - hi
    mid = rest.astype(bf16).astype(f32)
    return hi, mid, rest - mid


def stack_rows(rows, width):
    r = lax.broadcasted_iota(jnp.int32, (16, width), 0)
    out = jnp.zeros((16, width), f32)
    for i, v in enumerate(rows):
        out = jnp.where(r == i, v, out)
    return out.astype(bf16)


def kernel(
    ts_ref, ggain_ref, ngain_ref, feat_hbm, convw_hbm, timew_hbm, qkvw_hbm, outw_hbm, cot_hbm,
    upd_out, fin_out,
    fext, convw, timew, qkvw, outw, cot, wq, wo, cols, hid, stat, xsend, x, s_buf, m_buf,
    at_send, at, g_send, g, part, other, zs, fin, z_own, m_own,
    local_sem, stat_ss, stat_rs, halo_ss, halo_rs, x_ss, x_rs, at_ss, at_rs, g_ss, g_rs,
    cot_ss, cot_rs, part_ss, part_rs, zs_ss, zs_rs, ag_ss, ag_rs, fin_ss, fin_rs, rest_ss, rest_rs, core_ss, core_rs, fin_sem,
):
    me = lax.axis_index("sp")
    dp = lax.axis_index("dp")

    def sp_peer(t):
        return lax.rem(me + t, NSP)

    y, z, core = me // 4, lax.rem(me // 2, 2), lax.rem(me, 2)
    zh, xi = dp // 4, lax.rem(dp, 4)

    chip = me // 2

    def x_peer(t):
        return zh * 4 + lax.rem(xi + t, 4)

    def zh_peer(t):
        return lax.rem(zh + t, 4) * 4 + xi

    def slab(dy, dz, dc):
        return lax.rem(y + dy, 4) * 4 + lax.rem(z + dz, 2) * 2 + lax.rem(core + dc, 2)

    def to_sp(src, dst, ss, rs_, j):
        return pltpu.make_async_remote_copy(
            src_ref=src, dst_ref=dst, send_sem=ss, recv_sem=rs_, device_id={"sp": j},
            device_id_type=pl.DeviceIdType.MESH)

    def to_dp(src, dst, ss, rs_, j):
        return pltpu.make_async_remote_copy(
            src_ref=src, dst_ref=dst, send_sem=ss, recv_sem=rs_, device_id={"dp": j},
            device_id_type=pl.DeviceIdType.MESH)

    def loop(lo, hi, body):
        def step(i, c):
            body(i)
            return c
        lax.fori_loop(lo, hi, step, 0)

    def fetch(i, src, dst):
        c = pltpu.make_async_copy(src, dst, local_sem.at[i])
        c.start()
        return c
    get_feat = fetch(0, feat_hbm, fext.at[W:W + T])

    barrier = pltpu.get_barrier_semaphore()

    def greet(t):
        pl.semaphore_signal(barrier, inc=1, device_id={"sp": sp_peer(t)},
                            device_id_type=pl.DeviceIdType.MESH)

    for t in range(1, 4):
        pl.semaphore_signal(barrier, inc=1, device_id={"dp": zh_peer(t)},
                            device_id_type=pl.DeviceIdType.MESH)
    for t in range(1, 4):
        for c in range(NSP // 2):
            pl.semaphore_signal(barrier, inc=1, device_id={"dp": x_peer(t), "sp": 2 * c + core},
                                device_id_type=pl.DeviceIdType.MESH)
    loop(1, NSP, greet)

    chan = lax.broadcasted_iota(jnp.int32, (C, L), 0)
    grp = lax.broadcasted_iota(jnp.int32, (C, L), 1)
    per_group = C // GROUPS
    member = ((chan >= grp * per_group) & (chan < grp * per_group + per_group))
    member = member.astype(f32).astype(bf16)
    get_feat.wait()
    get_timew = fetch(1, timew_hbm, timew)
    get_qkvw = fetch(2, qkvw_hbm, qkvw)
    get_outw = fetch(4, outw_hbm, outw)
    get_convw = fetch(3, convw_hbm, convw)
    get_cot = fetch(5, cot_hbm, cot.at[core])
    feats = fext[W:W + T].astype(f32)
    s1 = jnp.sum(feats, axis=0, keepdims=True)
    s2 = jnp.sum(feats * feats, axis=0, keepdims=True)
    parts = jnp.dot(stack_rows(split3(s1) + split3(s2), C), member, preferred_element_type=f32)
    r8 = lax.broadcasted_iota(jnp.int32, (8, L), 0)
    t1 = parts[0:1] + parts[1:2] + parts[2:3]
    t2 = parts[3:4] + parts[4:5] + parts[5:6]
    stat[me] = jnp.where(r8 == 0, t1, jnp.where(r8 == 1, t2, 0.0))

    pl.semaphore_wait(barrier, NSP - 1 + 3 + 3 * NSP // 2)

    loop(1, NSP, lambda t: to_sp(
        stat.at[me], stat.at[me], stat_ss.at[sp_peer(t)], stat_rs.at[me], sp_peer(t)).start())
    up = to_sp(fext.at[W:2 * W], fext.at[3 * W:4 * W], halo_ss.at[0], halo_rs.at[0],
               lax.max(me - 1, 0))
    down = to_sp(fext.at[2 * W:3 * W], fext.at[0:W], halo_ss.at[1], halo_rs.at[1],
                 lax.min(me + 1, NSP - 1))

    @pl.when(me > 0)
    def _():
        up.start()

    @pl.when(me < NSP - 1)
    def _():
        down.start()

    sibling = slab(0, 0, 1)
    swap_cot = to_sp(cot.at[core], cot.at[core], cot_ss.at[0], cot_rs.at[0], sibling)

    get_timew.wait()
    half = TEMB // 2
    ti = lax.broadcasted_iota(jnp.int32, (8, TEMB), 1)
    tf = jnp.where(ti < half, ti, ti - half).astype(f32)
    freq = jnp.exp(-math.log(10000.0) * tf / half)
    angle = ts_ref[...].astype(f32).reshape(1, 1) * freq
    emb = jnp.where(ti < half, jnp.cos(angle), jnp.sin(angle))
    emb = emb / (1.0 + jnp.exp(-emb))
    time_bias = jnp.dot(emb.astype(bf16), timew[...], preferred_element_type=f32)[0:1]

    get_qkvw.wait()
    lane = lax.broadcasted_iota(jnp.int32, (1, L), 1)

    def regroup(r):
        here = pl.ds(pl.multiple_of(r * L, L), L)
        for j in range(HEADS):
            base = (3 * HD * j) // L * L
            off = 3 * HD * j - base
            width = 2 * L if 0 < off and base + 2 * L <= 3 * C else L
            piece = qkvw[here, base:base + width].astype(f32)
            if off:
                piece = pltpu.roll(piece, width - off, axis=1)[:, :L]
            piece = jnp.where(lane < 3 * HD, piece, 0.0).astype(bf16)
            wq[j // 2, here, (j % 2) * L:(j % 2) * L + L] = piece
    loop(0, C // L, regroup)
    get_outw.wait()
    for j in range(HEADS):
        if (HD * j) % 16 == 0:
            rows = outw[HD * j:HD * j + HP] if j < HEADS - 1 else outw[HD * j:HD * j + HD]
            rows = rows.astype(f32)[:HD]
        else:
            rows = outw[HD * j - 8:HD * j + HD].astype(f32)[8:]
        here = slice(HP * (j // 2), HP * (j // 2) + HP)
        wo[j % 2, here] = jnp.concatenate(
            [rows, jnp.zeros((HP - HD, C), f32)], axis=0).astype(bf16)

    loop(1, NSP, lambda t: to_sp(
        stat.at[sp_peer(t)], stat.at[sp_peer(t)], stat_ss.at[sp_peer(t)],
        stat_rs.at[sp_peer(t)], sp_peer(t)).wait_recv())
    total = jnp.sum(stat[...], axis=0)
    cells = float(NSP * T * per_group)
    mean = total[0:1] / cells
    rstd = lax.rsqrt(total[1:2] / cells - mean * mean + 1e-5)
    chan_t = lax.broadcasted_iota(jnp.int32, (L, C), 1)
    grp_t = lax.broadcasted_iota(jnp.int32, (L, C), 0)
    member_t = ((chan_t >= grp_t * per_group) & (chan_t < grp_t * per_group + per_group))
    member_t = member_t.astype(f32).astype(bf16)
    wide = jnp.dot(stack_rows(split3(mean) + split3(rstd), L), member_t,
                   preferred_element_type=f32)
    mean_c = wide[0:1] + wide[1:2] + wide[2:3]
    rstd_c = wide[3:4] + wide[4:5] + wide[5:6]
    col = lax.broadcasted_iota(jnp.int32, (W, C), 0)

    def activate(r, keep):
        here = pl.ds(pl.multiple_of(r * W, W), W)
        v = (fext[here].astype(f32) - mean_c) * rstd_c * ggain_ref[...].reshape(1, C)
        a = v / (1.0 + jnp.exp(-v))
        a = jnp.where(keep, a, 0.0)
        cols[here, 0:C] = jnp.where(col == 0, 0.0, pltpu.roll(a, 1, axis=0)).astype(bf16)
        cols[here, C:2 * C] = a.astype(bf16)
        cols[here, 2 * C:3 * C] = jnp.where(
            col == W - 1, 0.0, pltpu.roll(a, W - 1, axis=0)).astype(bf16)

    loop(1, 3, lambda r: activate(r, r > 0))

    @pl.when(me > 0)
    def _():
        down.wait_recv()

    @pl.when(me == 0)
    def _():
        fext[0:W] = jnp.zeros((W, C), bf16)

    @pl.when(me < NSP - 1)
    def _():
        up.wait_recv()

    @pl.when(me == NSP - 1)
    def _():
        fext[3 * W:4 * W] = jnp.zeros((W, C), bf16)

    loop(0, 2, lambda r: activate(3 * r, jnp.where(r == 0, me > 0, me < NSP - 1)))

    get_convw.wait()
    get_cot.wait()
    swap_cot.start()
    conv = fext[W:W + T].astype(f32) + time_bias
    for a in range(3):
        conv = conv + jnp.dot(cols[a * W:a * W + T], convw[a], preferred_element_type=f32)
    hidden = conv.astype(bf16)
    hid[...] = hidden
    h = hidden.astype(f32)
    centred = h - jnp.mean(h, axis=1, keepdims=True)
    variance = jnp.mean(centred * centred, axis=1, keepdims=True)
    normed = (centred * lax.rsqrt(variance + 1e-5) * ngain_ref[...].reshape(1, C)).astype(bf16)

    scale = jnp.where(lane < HD, math.log2(math.e) / math.sqrt(HD), 1.0)
    ones = jnp.where(lane >= 3 * HD, 1.0, 0.0)

    def send_x(j):
        return to_sp(xsend.at[j], x.at[me], x_ss.at[j], x_rs.at[me], j)

    for dy, dz in ((0, 1), (1, 0), (3, 0), (2, 0), (0, 0), (1, 1), (3, 1), (2, 1)):
        there = slab(dy, dz, 0) // 2
        pair = jnp.dot(normed, wq[there], preferred_element_type=f32)
        for k in range(2):
            xsend[2 * there + k] = (pair[:, k * L:(k + 1) * L] * scale + ones).astype(bf16)
        if dy == 0 and dz == 0:
            send_x(slab(0, 0, 1)).start()
            x[me] = xsend[me]
        else:
            for k in range(2):
                send_x(2 * there + k).start()

    def recv_x(j):
        to_sp(x.at[j], x.at[j], x_ss.at[j], x_rs.at[j], j).wait_recv()
    for dy in range(4):
        for dc in range(2):
            if dy or dc:
                recv_x(slab(dy, 0, dc))

    def query(j):
        q = pltpu.roll(x[j].astype(f32), HD, axis=1)
        return jnp.where((lane >= HD) & (lane < 2 * HD), q, 0.0).astype(bf16)

    def keys(kind, c):
        first = {"all": 2 * c, "own": 4 * c + 2 * z, "other": 4 * c + 2 * (1 - z)}[kind]
        return x[pl.ds(first, 2)].reshape(2 * T, L)

    chunks = {"all": NSP // 2, "own": NSP // 4, "other": NSP // 4}

    def scores(q, kind, buf, c, top):
        s = lax.dot_general(q, keys(kind, c), NT, preferred_element_type=f32)
        s_buf[buf, :, c * CK:(c + 1) * CK] = s
        for i in range(CK // L):
            top = jnp.maximum(top, s[:, i * L:(i + 1) * L])
        return top

    def weigh(m, kind, buf, c, acc):
        p = jnp.exp2(s_buf[buf, :, c * CK:(c + 1) * CK] - m).astype(bf16)
        return acc + jnp.dot(p, keys(kind, c), preferred_element_type=f32)

    lowest = jnp.full((T, L), -jnp.inf, f32)
    hrow = lax.broadcasted_iota(jnp.int32, (HP, T), 0)

    def begin(q, kind):
        top = lowest
        for c in range(chunks[kind]):
            top = scores(q, kind, 0, c, top)
        m_buf[...] = top

    def attend(kind, buf, nxt, before=None):
        m = jnp.max(m_buf[...], axis=1, keepdims=True)
        if before is None:
            acc = jnp.zeros((T, L), f32)
        else:
            m0 = m_own[before][:, :1]
            m = jnp.maximum(m, m0)
            acc = z_own[before] * jnp.exp2(m0 - m)
        top = lowest
        for c in range(NSP // 2):
            if nxt is not None and c < chunks[nxt[1]]:
                top = scores(nxt[0], nxt[1], 1 - buf, c, top)
            if c < chunks[kind]:
                acc = weigh(m, kind, buf, c, acc)
        if nxt is not None:
            m_buf[...] = top
        return acc, m

    def finish(acc):
        at_t = (acc / acc[:, 3 * HD:3 * HD + 1]).T[2 * HD:]
        return jnp.where(hrow < HD, at_t, 0.0).astype(bf16)

    def dy_of(p):
        k = lax.rem(p, 4)
        return lax.select(k == 0, 2, lax.select(k == 1, 1, lax.select(k == 2, 3, 0)))

    def target(p):
        return slab(dy_of(p), 1 - p // 4, 0) // 2

    def source(p):
        return slab(4 - dy_of(p), 1 - p // 4, 0) // 2

    def send_at(c):
        return to_sp(at_send.at[c], at.at[chip], at_ss.at[c], at_rs.at[chip], 2 * c + core)

    def recv_at(c):
        return to_sp(at.at[c], at.at[c], at_ss.at[c], at_rs.at[c], 2 * c + core)

    def send_g(c, k):
        return pltpu.make_async_remote_copy(
            src_ref=g_send.at[c, k], dst_ref=g.at[xi, chip], send_sem=g_ss.at[c, k],
            recv_sem=g_rs.at[xi, chip], device_id={"dp": zh * 4 + k, "sp": 2 * c + core},
            device_id_type=pl.DeviceIdType.MESH)

    def put_g(c, rows):
        low = [rows[32:HD, L * b:L * b + L] for b in range(5)] + [jnp.zeros((8, L), f32)]
        for i in range(12):
            if i < 10:
                tile = rows[16 * (i // 5):16 * (i // 5) + 16, L * (i % 5):L * (i % 5) + L]
            else:
                tile = jnp.concatenate(low[2 * i - 20:2 * i - 18], axis=0)
            g_send[c, i // 3, 16 * (i % 3):16 * (i % 3) + 16] = tile.astype(bf16)
        spare = jnp.concatenate(low[4:], axis=0).astype(bf16)
        for k in range(4):
            g_send[c, k, 48:64] = spare

    def i32(v):
        return jnp.int32(v)

    begin(query(2 * target(i32(4))), "own")

    def own_pair(u):
        now, later = target(4 + u), target(4 + lax.rem(u + 1, 4))
        for k in range(2):
            acc, m = attend("own", k, (query(2 * now + 1 if k == 0 else 2 * later), "own"))
            z_own[2 * u + k] = acc
            m_own[2 * u + k] = jnp.broadcast_to(m, (T, L))
    loop(0, 4, own_pair)

    for dy in range(4):
        for dc in range(2):
            recv_x(slab(dy, 1, dc))
    swap_cot.wait_recv()
    cots = cot.reshape(2 * T, C)

    def grads(p):
        c = source(p)
        recv_at(c).wait_recv()
        put_g(c, jnp.dot(at[c], cots[...], preferred_element_type=f32))

        def start():
            for k in range(4):
                send_g(c, k).start()
        return start

    begin(query(2 * target(i32(0))), "all")

    def cross_pair(u, last):
        now, later = target(u), target(u + 1)
        acc, _ = attend("all", 0, (query(2 * now + 1), "all"))
        at_send[now, :, 0:T] = finish(acc)
        acc, _ = attend("all", 1, (query(2 * later), "other" if last else "all"))
        at_send[now, :, T:2 * T] = finish(acc)
        send_at(now).start()
    loop(0, 3, lambda u: cross_pair(u, False))
    cross_pair(i32(3), True)

    def side_pair(u, last):
        start = grads(u)
        now, later = target(4 + u), target(4 + lax.rem(u + 1, 4))
        acc, _ = attend("other", 0, (query(2 * now + 1), "other"), before=2 * u)
        at_send[now, :, 0:T] = finish(acc)
        acc, _ = attend("other", 1, None if last else (query(2 * later), "other"),
                        before=2 * u + 1)
        at_send[now, :, T:2 * T] = finish(acc)
        if not last:
            send_at(now).start()
        start()
    loop(0, 3, lambda u: side_pair(u, False))
    side_pair(i32(3), True)

    at[chip] = at_send[chip]
    last = [source(i32(p)) for p in (4, 5, 6)]
    for c in last:
        recv_at(c).wait_recv()
    block = jnp.concatenate([at[c] for c in last] + [at[chip]], axis=0)
    final = jnp.dot(block, cots[...], preferred_element_type=f32)
    for i, c in enumerate(last):
        put_g(c, final[i * HP:(i + 1) * HP])
        for k in range(4):
            send_g(c, k).start()
    put_g(chip, final[3 * HP:])
    for t in range(1, 4):
        send_g(chip, lax.rem(xi + t, 4)).start()
    g[xi, chip] = g_send[chip, xi]

    def recv_g(t):
        k, c = lax.rem(xi + t // 8, 4), lax.rem(chip + t, 8)
        pltpu.make_async_remote_copy(
            src_ref=g.at[k, c], dst_ref=g.at[k, c], send_sem=g_ss.at[c, k],
            recv_sem=g_rs.at[k, c], device_id={"dp": zh * 4 + k, "sp": 2 * c + core},
            device_id_type=pl.DeviceIdType.MESH).wait_recv()
    loop(1, 4 * NSP // 2, recv_g)

    def add_g(k, total):
        return total + jnp.sum(g[k].astype(f32), axis=0)

    def send_zs(t):
        return to_dp(zs.at[zh], zs.at[zh], zs_ss.at[t], zs_rs.at[zh], zh_peer(t))
    zs[zh] = lax.fori_loop(0, 4, add_g, jnp.zeros((64, L), f32)).astype(bf16)
    for t in (2, 1, 3):
        send_zs(t).start()

    mixed = lax.dot_general(at[...].reshape(NSP // 2 * HP, 2 * T), wo[core], TN,
                            preferred_element_type=f32)
    part[0] = mixed[:T]
    part[1] = mixed[T:]
    swap_part = to_sp(part.at[1 - core], other, part_ss.at[0], part_rs.at[0], sibling)
    swap_part.start()

    @pl.when(me > 0)
    def _():
        up.wait_send()

    @pl.when(me < NSP - 1)
    def _():
        down.wait_send()

    def drain(t):
        j = sp_peer(t)
        to_sp(stat.at[me], stat.at[me], stat_ss.at[j], stat_rs.at[me], j).wait_send()
        send_x(j).wait_send()
    loop(1, NSP, drain)

    def drain_pair(t):
        c = lax.rem(chip + t, NSP // 2)
        send_at(c).wait_send()
        for k in range(4):
            send_g(c, k).wait_send()
    loop(1, NSP // 2, drain_pair)
    swap_cot.wait_send()
    for t in range(1, 4):
        send_g(chip, lax.rem(xi + t, 4)).wait_send()

    for t in (1, 3, 2):
        k = lax.rem(zh + t, 4)
        to_dp(zs.at[k], zs.at[k], zs_ss.at[t], zs_rs.at[k], zh_peer(t)).wait_recv()
    fin[me, 0:64] = jnp.sum(zs[...].astype(f32), axis=0).astype(bf16)

    def send_ag(t):
        return to_dp(fin.at[me, pl.ds(0, 48)], fin.at[me, pl.ds(64 + 48 * (3 - t), 48)],
                     ag_ss.at[t], ag_rs.at[4 - t], x_peer(t))

    def send_own(u):
        j = lax.rem(me + 2 * u, NSP)
        return to_sp(fin.at[me, pl.ds(0, 64)], fin.at[me, pl.ds(0, 64)], fin_ss.at[j],
                     fin_rs.at[me], j)

    def send_rest(u):
        j = lax.rem(me + 2 * u, NSP)
        return to_sp(fin.at[me, pl.ds(64, 144)], fin.at[me, pl.ds(64, 144)], rest_ss.at[j],
                     rest_rs.at[me], j)
    def pass_on(j):
        return to_sp(fin.at[j], fin.at[j], core_ss.at[j], core_rs.at[j], sibling)
    for t in (2, 1, 3):
        send_ag(t).start()
    loop(1, NSP // 2, lambda u: send_own(u).start())
    swap_part.wait_recv()
    hid[...] = (hid[...].astype(f32) + part[core] + other[...]).astype(bf16)
    put_upd = pltpu.make_async_copy(hid, upd_out, local_sem.at[0])
    put_upd.start()

    for k in (1, 3, 2):
        quarter = fin.at[me, pl.ds(64 + 48 * (k - 1), 48)]
        to_dp(quarter, quarter, ag_ss.at[k], ag_rs.at[k], x_peer(k)).wait_recv()
    loop(1, NSP // 2, lambda u: send_rest(u).start())
    pass_on(me).start()

    def put_fin(j):
        return pltpu.make_async_copy(fin.at[j], fin_out.at[j], fin_sem.at[j])
    put_fin(me).start()
    swap_part.wait_send()
    for t in range(1, 4):
        send_zs(t).wait_send()
        send_ag(t).wait_send()
    loop(1, NSP // 2, lambda u: send_own(u).wait_send())

    def relay(u):
        j = lax.rem(me + NSP - 2 * u, NSP)
        own, rest = fin.at[j, pl.ds(0, 64)], fin.at[j, pl.ds(64, 144)]
        to_sp(own, own, fin_ss.at[j], fin_rs.at[j], j).wait_recv()
        to_sp(rest, rest, rest_ss.at[j], rest_rs.at[j], j).wait_recv()
        pass_on(j).start()
        put_fin(j).start()
    loop(1, NSP // 2, relay)
    loop(1, NSP // 2, lambda u: send_rest(u).wait_send())

    def recv_core(u):
        j = lax.rem(sibling + NSP - 2 * u, NSP)
        to_sp(fin.at[j], fin.at[j], core_ss.at[j], core_rs.at[j], sibling).wait_recv()
        put_fin(j).start()
    loop(0, NSP // 2, recv_core)

    loop(1, NSP // 2, lambda u: pass_on(lax.rem(me + NSP - 2 * u, NSP)).wait_send())
    pass_on(me).wait_send()
    put_upd.wait()
    loop(0, NSP, lambda j: put_fin(j).wait())


def outputs(fin_hbm, upd_hbm, upd_out, grad_out, fin, upd, grad, sem):
    xi = lax.rem(lax.axis_index("dp"), 4)
    take = pltpu.make_async_copy(upd_hbm, upd, sem.at[HEADS // 2])
    move = pltpu.make_async_copy(upd, upd_out, sem.at[HEADS // 2])

    def get(j):
        return pltpu.make_async_copy(fin_hbm.at[pl.ds(j, 2)], fin.at[pl.ds(j, 2)],
                                     sem.at[HEADS // 2 + 1 + j // 2])
    for j in range(0, HEADS, 2):
        get(j).start()
    take.start()
    turn = [lax.rem(k + 4 - xi, 4) for k in range(4)]
    start = [pl.multiple_of(lax.select(r == 0, 0, 16 + 48 * r), 16) for r in turn]

    def head_rows(j):
        tiles = [fin[j, pl.ds(start[i // 3] + 16 * (i % 3), 16)].astype(f32) for i in range(12)]
        spare = fin[j, 48:64].astype(f32)
        low = [tiles[10][:8], tiles[10][8:], tiles[11][:8], tiles[11][8:], spare[:8]]
        return [jnp.concatenate(row, axis=1) for row in (tiles[:5], tiles[5:10], low)]
    for j in range(0, HEADS, 2):
        get(j).wait()
        two = jnp.concatenate(head_rows(j) + head_rows(j + 1), axis=0)
        here = slice(HD * j, HD * j + 2 * HD)
        grad[here] = two
        pltpu.make_async_copy(grad.at[here], grad_out.at[here], sem.at[j // 2]).start()
    take.wait()
    move.start()
    for j in range(0, HEADS, 2):
        here = slice(HD * j, HD * j + 2 * HD)
        pltpu.make_async_copy(grad.at[here], grad_out.at[here], sem.at[j // 2]).wait()
    move.wait()


def on_device(features, timestep, group_gain, conv_weight, time_weight, norm_gain, qkv_weight,
              out_weight, cotangent):
    vmem = pl.BlockSpec(memory_space=pltpu.VMEM)
    hbm = pl.BlockSpec(memory_space=pl.ANY)
    dma = pltpu.SemaphoreType.DMA
    updated, tiles = pl.pallas_call(
        kernel,
        out_shape=(
            jax.ShapeDtypeStruct((T, C), bf16),
            jax.ShapeDtypeStruct((NSP, 13 * 16, L), bf16),
        ),
        in_specs=[vmem, vmem, vmem] + [hbm] * 6,
        out_specs=(hbm, hbm),
        scratch_shapes=[
            pltpu.VMEM((4 * W, C), bf16),
            pltpu.VMEM((3, 3 * C, C), bf16),
            pltpu.VMEM((TEMB, C), bf16),
            pltpu.VMEM((C, 3 * C), bf16),
            pltpu.VMEM((C, C), bf16),
            pltpu.VMEM((2, T, C), bf16),
            pltpu.VMEM((HEADS // 2, C, 2 * L), bf16),
            pltpu.VMEM((2, HEADS // 2 * HP, C), bf16),
            pltpu.VMEM((4 * W, 3 * C), bf16),
            pltpu.VMEM((T, C), bf16),
            pltpu.VMEM((NSP, 8, L), f32),
            pltpu.VMEM((NSP, T, L), bf16),
            pltpu.VMEM((NSP, T, L), bf16),
            pltpu.VMEM((2, T, NSP * T), f32),
            pltpu.VMEM((T, L), f32),
            pltpu.VMEM((NSP // 2, HP, 2 * T), bf16),
            pltpu.VMEM((NSP // 2, HP, 2 * T), bf16),
            pltpu.VMEM((NSP // 2, 4, 64, L), bf16),
            pltpu.VMEM((4, NSP // 2, 64, L), bf16),
            pltpu.VMEM((2, T, C), f32),
            pltpu.VMEM((T, C), f32),
            pltpu.VMEM((4, 64, L), bf16),
            pltpu.VMEM((NSP, 13 * 16, L), bf16),
            pltpu.VMEM((8, T, L), f32),
            pltpu.VMEM((8, T, L), f32),
            dma((6,)), dma((16,)), dma((16,)), dma((2,)), dma((2,)), dma((16,)), dma((16,)),
            dma((8,)), dma((8,)), dma((8, 4)), dma((4, 8)),
            dma((1,)), dma((1,)), dma((1,)), dma((1,)),
            dma((4,)), dma((4,)), dma((4,)), dma((4,)),
            dma((16,)), dma((16,)), dma((16,)), dma((16,)), dma((16,)), dma((16,)), dma((16,)),
        ],
        compiler_params=pltpu.CompilerParams(
            collective_id=0, has_side_effects=True, vmem_limit_bytes=60 * 2**20),
        name="level",
    )(
        timestep, group_gain, norm_gain, features.reshape(T, C),
        conv_weight.reshape(3, 3 * C, C), time_weight, qkv_weight, out_weight,
        cotangent.reshape(T, C),
    )
    updated, out_grad = pl.pallas_call(
        outputs,
        out_shape=(
            jax.ShapeDtypeStruct((T, C), bf16),
            jax.ShapeDtypeStruct((C, C), f32),
        ),
        in_specs=[hbm, hbm],
        out_specs=(hbm, hbm),
        scratch_shapes=[
            pltpu.VMEM((NSP, 13 * 16, L), bf16),
            pltpu.VMEM((T, C), bf16),
            pltpu.VMEM((C, C), f32),
            dma((HEADS + 1,)),
        ],
        compiler_params=pltpu.CompilerParams(vmem_limit_bytes=63 * 2**20),
        name="outputs",
    )(tiles, updated)
    return updated.reshape(1, ROWS, W, C), out_grad


def solution(mesh):
    slab = P("dp", "sp", None, None)
    return jax.shard_map(
        on_device, mesh=mesh,
        in_specs=(slab, P("dp"), P(), P(), P(), P(), P(), P(), slab),
        out_specs=(slab, P()), check_vma=False,
    )
```

```python
import functools
import math

import jax
import jax.numpy as jnp
from jax import lax
from jax.experimental import pallas as pl
from jax.experimental.pallas import tpu as pltpu
from jax.sharding import PartitionSpec as P

HEADS = 16
GROUPS = 32
C = 640
HD = 40
W = 128
TEMB = 320
ROWS = 2
T = ROWS * W
L = 128
HP = 48
NSP = 16
NDP = 16
f32 = jnp.float32
bf16 = jnp.bfloat16
NT = (((1,), (1,)), ((), ()))
TN = (((0,), (0,)), ((), ()))
CK = 512


def split3(v):
    hi = v.astype(bf16).astype(f32)
    rest = v - hi
    mid = rest.astype(bf16).astype(f32)
    return hi, mid, rest - mid


def stack_rows(rows, width):
    r = lax.broadcasted_iota(jnp.int32, (16, width), 0)
    out = jnp.zeros((16, width), f32)
    for i, v in enumerate(rows):
        out = jnp.where(r == i, v, out)
    return out.astype(bf16)


def kernel(
    ts_ref, ggain_ref, ngain_ref, feat_hbm, convw_hbm, timew_hbm, qkvw_hbm, outw_hbm, cot_hbm,
    upd_out, fin_out,
    fext, convw, timew, qkvw, outw, cot, wq, wo, cols, hid, stat, xsend, x, s_buf, m_buf,
    at_send, at, g_send, g, part, other, zs, fin, z_own, m_own,
    local_sem, stat_ss, stat_rs, halo_ss, halo_rs, x_ss, x_rs, at_ss, at_rs, g_ss, g_rs,
    cot_ss, cot_rs, part_ss, part_rs, zs_ss, zs_rs, ag_ss, ag_rs, fin_ss, fin_rs, rest_ss, rest_rs, core_ss, core_rs, fin_sem,
):
    me = lax.axis_index("sp")
    dp = lax.axis_index("dp")

    def sp_peer(t):
        return lax.rem(me + t, NSP)

    y, z, core = me // 4, lax.rem(me // 2, 2), lax.rem(me, 2)
    zh, xi = dp // 4, lax.rem(dp, 4)

    chip = me // 2

    def x_peer(t):
        return zh * 4 + lax.rem(xi + t, 4)

    def zh_peer(t):
        return lax.rem(zh + t, 4) * 4 + xi

    def slab(dy, dz, dc):
        return lax.rem(y + dy, 4) * 4 + lax.rem(z + dz, 2) * 2 + lax.rem(core + dc, 2)

    def to_sp(src, dst, ss, rs_, j):
        return pltpu.make_async_remote_copy(
            src_ref=src, dst_ref=dst, send_sem=ss, recv_sem=rs_, device_id={"sp": j},
            device_id_type=pl.DeviceIdType.MESH)

    def to_dp(src, dst, ss, rs_, j):
        return pltpu.make_async_remote_copy(
            src_ref=src, dst_ref=dst, send_sem=ss, recv_sem=rs_, device_id={"dp": j},
            device_id_type=pl.DeviceIdType.MESH)

    def loop(lo, hi, body):
        def step(i, c):
            body(i)
            return c
        lax.fori_loop(lo, hi, step, 0)

    def fetch(i, src, dst):
        c = pltpu.make_async_copy(src, dst, local_sem.at[i])
        c.start()
        return c
    get_feat = fetch(0, feat_hbm, fext.at[W:W + T])

    barrier = pltpu.get_barrier_semaphore()

    def greet(t):
        pl.semaphore_signal(barrier, inc=1, device_id={"sp": sp_peer(t)},
                            device_id_type=pl.DeviceIdType.MESH)

    for t in range(1, 4):
        pl.semaphore_signal(barrier, inc=1, device_id={"dp": zh_peer(t)},
                            device_id_type=pl.DeviceIdType.MESH)
    for t in range(1, 4):
        for c in range(NSP // 2):
            pl.semaphore_signal(barrier, inc=1, device_id={"dp": x_peer(t), "sp": 2 * c + core},
                                device_id_type=pl.DeviceIdType.MESH)
    loop(1, NSP, greet)

    chan = lax.broadcasted_iota(jnp.int32, (C, L), 0)
    grp = lax.broadcasted_iota(jnp.int32, (C, L), 1)
    per_group = C // GROUPS
    member = ((chan >= grp * per_group) & (chan < grp * per_group + per_group))
    member = member.astype(f32).astype(bf16)
    get_feat.wait()
    get_timew = fetch(1, timew_hbm, timew)
    get_qkvw = fetch(2, qkvw_hbm, qkvw)
    get_outw = fetch(4, outw_hbm, outw)
    get_convw = fetch(3, convw_hbm, convw)
    get_cot = fetch(5, cot_hbm, cot.at[core])
    feats = fext[W:W + T].astype(f32)
    s1 = jnp.sum(feats, axis=0, keepdims=True)
    s2 = jnp.sum(feats * feats, axis=0, keepdims=True)
    parts = jnp.dot(stack_rows(split3(s1) + split3(s2), C), member, preferred_element_type=f32)
    r8 = lax.broadcasted_iota(jnp.int32, (8, L), 0)
    t1 = parts[0:1] + parts[1:2] + parts[2:3]
    t2 = parts[3:4] + parts[4:5] + parts[5:6]
    stat[me] = jnp.where(r8 == 0, t1, jnp.where(r8 == 1, t2, 0.0))

    pl.semaphore_wait(barrier, NSP - 1 + 3 + 3 * NSP // 2)

    loop(1, NSP, lambda t: to_sp(
        stat.at[me], stat.at[me], stat_ss.at[sp_peer(t)], stat_rs.at[me], sp_peer(t)).start())
    up = to_sp(fext.at[W:2 * W], fext.at[3 * W:4 * W], halo_ss.at[0], halo_rs.at[0],
               lax.max(me - 1, 0))
    down = to_sp(fext.at[2 * W:3 * W], fext.at[0:W], halo_ss.at[1], halo_rs.at[1],
                 lax.min(me + 1, NSP - 1))

    @pl.when(me > 0)
    def _():
        up.start()

    @pl.when(me < NSP - 1)
    def _():
        down.start()

    sibling = slab(0, 0, 1)
    swap_cot = to_sp(cot.at[core], cot.at[core], cot_ss.at[0], cot_rs.at[0], sibling)

    get_timew.wait()
    half = TEMB // 2
    ti = lax.broadcasted_iota(jnp.int32, (8, TEMB), 1)
    tf = jnp.where(ti < half, ti, ti - half).astype(f32)
    freq = jnp.exp(-math.log(10000.0) * tf / half)
    angle = ts_ref[...].astype(f32).reshape(1, 1) * freq
    emb = jnp.where(ti < half, jnp.cos(angle), jnp.sin(angle))
    emb = emb / (1.0 + jnp.exp(-emb))
    time_bias = jnp.dot(emb.astype(bf16), timew[...], preferred_element_type=f32)[0:1]

    get_qkvw.wait()
    lane = lax.broadcasted_iota(jnp.int32, (1, L), 1)

    def regroup(r):
        here = pl.ds(pl.multiple_of(r * L, L), L)
        for j in range(HEADS):
            base = (3 * HD * j) // L * L
            off = 3 * HD * j - base
            width = 2 * L if 0 < off and base + 2 * L <= 3 * C else L
            piece = qkvw[here, base:base + width].astype(f32)
            if off:
                piece = pltpu.roll(piece, width - off, axis=1)[:, :L]
            piece = jnp.where(lane < 3 * HD, piece, 0.0).astype(bf16)
            wq[j // 2, here, (j % 2) * L:(j % 2) * L + L] = piece
    loop(0, C // L, regroup)

    loop(1, NSP, lambda t: to_sp(
        stat.at[sp_peer(t)], stat.at[sp_peer(t)], stat_ss.at[sp_peer(t)],
        stat_rs.at[sp_peer(t)], sp_peer(t)).wait_recv())
    total = jnp.sum(stat[...], axis=0)
    cells = float(NSP * T * per_group)
    mean = total[0:1] / cells
    rstd = lax.rsqrt(total[1:2] / cells - mean * mean + 1e-5)
    chan_t = lax.broadcasted_iota(jnp.int32, (L, C), 1)
    grp_t = lax.broadcasted_iota(jnp.int32, (L, C), 0)
    member_t = ((chan_t >= grp_t * per_group) & (chan_t < grp_t * per_group + per_group))
    member_t = member_t.astype(f32).astype(bf16)
    wide = jnp.dot(stack_rows(split3(mean) + split3(rstd), L), member_t,
                   preferred_element_type=f32)
    mean_c = wide[0:1] + wide[1:2] + wide[2:3]
    rstd_c = wide[3:4] + wide[4:5] + wide[5:6]
    col = lax.broadcasted_iota(jnp.int32, (W, C), 0)

    def activate(r, keep):
        here = pl.ds(pl.multiple_of(r * W, W), W)
        v = (fext[here].astype(f32) - mean_c) * rstd_c * ggain_ref[...].reshape(1, C)
        a = v / (1.0 + jnp.exp(-v))
        a = jnp.where(keep, a, 0.0)
        cols[here, 0:C] = jnp.where(col == 0, 0.0, pltpu.roll(a, 1, axis=0)).astype(bf16)
        cols[here, C:2 * C] = a.astype(bf16)
        cols[here, 2 * C:3 * C] = jnp.where(
            col == W - 1, 0.0, pltpu.roll(a, W - 1, axis=0)).astype(bf16)

    loop(1, 3, lambda r: activate(r, r > 0))

    @pl.when(me > 0)
    def _():
        down.wait_recv()

    @pl.when(me == 0)
    def _():
        fext[0:W] = jnp.zeros((W, C), bf16)

    @pl.when(me < NSP - 1)
    def _():
        up.wait_recv()

    @pl.when(me == NSP - 1)
    def _():
        fext[3 * W:4 * W] = jnp.zeros((W, C), bf16)

    loop(0, 2, lambda r: activate(3 * r, jnp.where(r == 0, me > 0, me < NSP - 1)))

    get_convw.wait()
    get_cot.wait()
    swap_cot.start()
    conv = fext[W:W + T].astype(f32) + time_bias
    for a in range(3):
        conv = conv + jnp.dot(cols[a * W:a * W + T], convw[a], preferred_element_type=f32)
    hidden = conv.astype(bf16)
    hid[...] = hidden
    h = hidden.astype(f32)
    centred = h - jnp.mean(h, axis=1, keepdims=True)
    variance = jnp.mean(centred * centred, axis=1, keepdims=True)
    normed = (centred * lax.rsqrt(variance + 1e-5) * ngain_ref[...].reshape(1, C)).astype(bf16)

    scale = jnp.where(lane < HD, math.log2(math.e) / math.sqrt(HD), 1.0)
    ones = jnp.where(lane >= 3 * HD, 1.0, 0.0)

    def send_x(j):
        return to_sp(xsend.at[j], x.at[me], x_ss.at[j], x_rs.at[me], j)

    for dy, dz in ((0, 1), (1, 0), (3, 0), (2, 0), (0, 0), (1, 1), (3, 1), (2, 1)):
        there = slab(dy, dz, 0) // 2
        pair = jnp.dot(normed, wq[there], preferred_element_type=f32)
        for k in range(2):
            xsend[2 * there + k] = (pair[:, k * L:(k + 1) * L] * scale + ones).astype(bf16)
        if dy == 0 and dz == 0:
            send_x(slab(0, 0, 1)).start()
            x[me] = xsend[me]
        else:
            for k in range(2):
                send_x(2 * there + k).start()

    def recv_x(j):
        to_sp(x.at[j], x.at[j], x_ss.at[j], x_rs.at[j], j).wait_recv()
    get_outw.wait()
    for j in range(HEADS):
        if (HD * j) % 16 == 0:
            rows = outw[HD * j:HD * j + HP] if j < HEADS - 1 else outw[HD * j:HD * j + HD]
            rows = rows.astype(f32)[:HD]
        else:
            rows = outw[HD * j - 8:HD * j + HD].astype(f32)[8:]
        here = slice(HP * (j // 2), HP * (j // 2) + HP)
        wo[j % 2, here] = jnp.concatenate(
            [rows, jnp.zeros((HP - HD, C), f32)], axis=0).astype(bf16)

    for dy in range(4):
        for dc in range(2):
            if dy or dc:
                recv_x(slab(dy, 0, dc))

    def query(j):
        q = pltpu.roll(x[j].astype(f32), HD, axis=1)
        return jnp.where((lane >= HD) & (lane < 2 * HD), q, 0.0).astype(bf16)

    def keys(kind, c):
        first = {"all": 2 * c, "own": 4 * c + 2 * z, "other": 4 * c + 2 * (1 - z)}[kind]
        return x[pl.ds(first, 2)].reshape(2 * T, L)

    chunks = {"all": NSP // 2, "own": NSP // 4, "other": NSP // 4}

    def scores(q, kind, buf, c, top):
        s = lax.dot_general(q, keys(kind, c), NT, preferred_element_type=f32)
        s_buf[buf, :, c * CK:(c + 1) * CK] = s
        for i in range(CK // L):
            top = jnp.maximum(top, s[:, i * L:(i + 1) * L])
        return top

    def weigh(m, kind, buf, c, acc):
        p = jnp.exp2(s_buf[buf, :, c * CK:(c + 1) * CK] - m).astype(bf16)
        return acc + jnp.dot(p, keys(kind, c), preferred_element_type=f32)

    lowest = jnp.full((T, L), -jnp.inf, f32)
    hrow = lax.broadcasted_iota(jnp.int32, (HP, T), 0)

    def begin(q, kind):
        top = lowest
        for c in range(chunks[kind]):
            top = scores(q, kind, 0, c, top)
        m_buf[...] = top

    def attend(kind, buf, nxt, before=None):
        m = jnp.max(m_buf[...], axis=1, keepdims=True)
        if before is None:
            acc = jnp.zeros((T, L), f32)
        else:
            m0 = m_own[before][:, :1]
            m = jnp.maximum(m, m0)
            acc = z_own[before] * jnp.exp2(m0 - m)
        top = lowest
        for c in range(NSP // 2):
            if nxt is not None and c < chunks[nxt[1]]:
                top = scores(nxt[0], nxt[1], 1 - buf, c, top)
            if c < chunks[kind]:
                acc = weigh(m, kind, buf, c, acc)
        if nxt is not None:
            m_buf[...] = top
        return acc, m

    def finish(acc):
        at_t = (acc / acc[:, 3 * HD:3 * HD + 1]).T[2 * HD:]
        return jnp.where(hrow < HD, at_t, 0.0).astype(bf16)

    def dy_of(p):
        k = lax.rem(p, 4)
        return lax.select(k == 0, 2, lax.select(k == 1, 1, lax.select(k == 2, 3, 0)))

    def target(p):
        return slab(dy_of(p), 1 - p // 4, 0) // 2

    def source(p):
        return slab(4 - dy_of(p), 1 - p // 4, 0) // 2

    def send_at(c):
        return to_sp(at_send.at[c], at.at[chip], at_ss.at[c], at_rs.at[chip], 2 * c + core)

    def recv_at(c):
        return to_sp(at.at[c], at.at[c], at_ss.at[c], at_rs.at[c], 2 * c + core)

    def send_g(c, k):
        return pltpu.make_async_remote_copy(
            src_ref=g_send.at[c, k], dst_ref=g.at[xi, chip], send_sem=g_ss.at[c, k],
            recv_sem=g_rs.at[xi, chip], device_id={"dp": zh * 4 + k, "sp": 2 * c + core},
            device_id_type=pl.DeviceIdType.MESH)

    def put_g(c, rows):
        low = [rows[32:HD, L * b:L * b + L] for b in range(5)] + [jnp.zeros((8, L), f32)]
        for i in range(12):
            if i < 10:
                tile = rows[16 * (i // 5):16 * (i // 5) + 16, L * (i % 5):L * (i % 5) + L]
            else:
                tile = jnp.concatenate(low[2 * i - 20:2 * i - 18], axis=0)
            g_send[c, i // 3, 16 * (i % 3):16 * (i % 3) + 16] = tile.astype(bf16)
        spare = jnp.concatenate(low[4:], axis=0).astype(bf16)
        for k in range(4):
            g_send[c, k, 48:64] = spare

    def i32(v):
        return jnp.int32(v)

    begin(query(2 * target(i32(4))), "own")

    def own_pair(u, last):
        now, later = target(4 + u), target(5 + u)
        for k in range(2):
            if k == 0:
                nxt = (query(2 * now + 1), "own")
            elif not last:
                nxt = (query(2 * later), "own")
            else:
                for dy in range(4):
                    for dc in range(2):
                        recv_x(slab(dy, 1, dc))
                nxt = (query(2 * target(i32(0))), "all")
            acc, m = attend("own", k, nxt)
            z_own[2 * u + k] = acc
            m_own[2 * u + k] = jnp.broadcast_to(m, (T, L))
    loop(0, 3, lambda u: own_pair(u, False))
    own_pair(i32(3), True)

    swap_cot.wait_recv()
    cots = cot.reshape(2 * T, C)

    def grads(p):
        c = source(p)
        recv_at(c).wait_recv()
        put_g(c, jnp.dot(at[c], cots[...], preferred_element_type=f32))

        def start():
            for k in range(4):
                send_g(c, k).start()
        return start

    def cross_pair(u, last):
        now, later = target(u), target(u + 1)
        acc, _ = attend("all", 0, (query(2 * now + 1), "all"))
        at_send[now, :, 0:T] = finish(acc)
        acc, _ = attend("all", 1, (query(2 * later), "other" if last else "all"))
        at_send[now, :, T:2 * T] = finish(acc)
        send_at(now).start()
    loop(0, 3, lambda u: cross_pair(u, False))
    cross_pair(i32(3), True)

    def side_pair(u, last):
        start = grads(u)
        now, later = target(4 + u), target(4 + lax.rem(u + 1, 4))
        acc, _ = attend("other", 0, (query(2 * now + 1), "other"), before=2 * u)
        at_send[now, :, 0:T] = finish(acc)
        acc, _ = attend("other", 1, None if last else (query(2 * later), "other"),
                        before=2 * u + 1)
        at_send[now, :, T:2 * T] = finish(acc)
        if not last:
            send_at(now).start()
        start()
    loop(0, 3, lambda u: side_pair(u, False))
    side_pair(i32(3), True)

    at[chip] = at_send[chip]
    last = [source(i32(p)) for p in (4, 5, 6)]
    for c in last[:2]:
        recv_at(c).wait_recv()
    block = jnp.concatenate([at[last[0]], at[last[1]], at[chip]], axis=0)
    final = jnp.dot(block, cots[...], preferred_element_type=f32)
    for i, c in enumerate(last[:2]):
        put_g(c, final[i * HP:(i + 1) * HP])
        for k in range(4):
            send_g(c, k).start()
    put_g(chip, final[2 * HP:])
    for t in range(1, 4):
        send_g(chip, lax.rem(xi + t, 4)).start()
    grads(i32(6))()
    g[xi, chip] = g_send[chip, xi]

    def recv_g(t):
        k, c = lax.rem(xi + t // 8, 4), lax.rem(chip + t, 8)
        pltpu.make_async_remote_copy(
            src_ref=g.at[k, c], dst_ref=g.at[k, c], send_sem=g_ss.at[c, k],
            recv_sem=g_rs.at[k, c], device_id={"dp": zh * 4 + k, "sp": 2 * c + core},
            device_id_type=pl.DeviceIdType.MESH).wait_recv()
    loop(1, 4 * NSP // 2, recv_g)

    def add_g(k, total):
        return total + jnp.sum(g[k].astype(f32), axis=0)

    def send_zs(t):
        return to_dp(zs.at[zh], zs.at[zh], zs_ss.at[t], zs_rs.at[zh], zh_peer(t))
    zs[zh] = lax.fori_loop(0, 4, add_g, jnp.zeros((64, L), f32)).astype(bf16)
    for t in (2, 1, 3):
        send_zs(t).start()

    mixed = lax.dot_general(at[...].reshape(NSP // 2 * HP, 2 * T), wo[core], TN,
                            preferred_element_type=f32)
    part[0] = mixed[:T]
    part[1] = mixed[T:]
    swap_part = to_sp(part.at[1 - core], other, part_ss.at[0], part_rs.at[0], sibling)
    swap_part.start()

    @pl.when(me > 0)
    def _():
        up.wait_send()

    @pl.when(me < NSP - 1)
    def _():
        down.wait_send()

    def drain(t):
        j = sp_peer(t)
        to_sp(stat.at[me], stat.at[me], stat_ss.at[j], stat_rs.at[me], j).wait_send()
        send_x(j).wait_send()
    loop(1, NSP, drain)

    def drain_pair(t):
        c = lax.rem(chip + t, NSP // 2)
        send_at(c).wait_send()
        for k in range(4):
            send_g(c, k).wait_send()
    loop(1, NSP // 2, drain_pair)
    swap_cot.wait_send()
    for t in range(1, 4):
        send_g(chip, lax.rem(xi + t, 4)).wait_send()

    for t in (1, 3, 2):
        k = lax.rem(zh + t, 4)
        to_dp(zs.at[k], zs.at[k], zs_ss.at[t], zs_rs.at[k], zh_peer(t)).wait_recv()
    fin[me, 0:64] = jnp.sum(zs[...].astype(f32), axis=0).astype(bf16)

    def send_ag(t):
        return to_dp(fin.at[me, pl.ds(0, 48)], fin.at[me, pl.ds(64 + 48 * (3 - t), 48)],
                     ag_ss.at[t], ag_rs.at[4 - t], x_peer(t))

    def send_own(u):
        j = lax.rem(me + 2 * u, NSP)
        return to_sp(fin.at[me, pl.ds(0, 64)], fin.at[me, pl.ds(0, 64)], fin_ss.at[j],
                     fin_rs.at[me], j)

    def send_rest(u):
        j = lax.rem(me + 2 * u, NSP)
        return to_sp(fin.at[me, pl.ds(64, 144)], fin.at[me, pl.ds(64, 144)], rest_ss.at[j],
                     rest_rs.at[me], j)
    def pass_on(j):
        return to_sp(fin.at[j], fin.at[j], core_ss.at[j], core_rs.at[j], sibling)
    for t in (2, 1, 3):
        send_ag(t).start()
    loop(1, NSP // 2, lambda u: send_own(u).start())
    swap_part.wait_recv()
    hid[...] = (hid[...].astype(f32) + part[core] + other[...]).astype(bf16)
    put_upd = pltpu.make_async_copy(hid, upd_out, local_sem.at[0])
    put_upd.start()

    for k in (1, 3, 2):
        quarter = fin.at[me, pl.ds(64 + 48 * (k - 1), 48)]
        to_dp(quarter, quarter, ag_ss.at[k], ag_rs.at[k], x_peer(k)).wait_recv()
    loop(1, NSP // 2, lambda u: send_rest(u).start())
    pass_on(me).start()

    def put_fin(j):
        return pltpu.make_async_copy(fin.at[j], fin_out.at[j], fin_sem.at[j])
    put_fin(me).start()
    swap_part.wait_send()
    for t in range(1, 4):
        send_zs(t).wait_send()
        send_ag(t).wait_send()
    loop(1, NSP // 2, lambda u: send_own(u).wait_send())

    def relay(u):
        j = lax.rem(me + NSP - 2 * u, NSP)
        own, rest = fin.at[j, pl.ds(0, 64)], fin.at[j, pl.ds(64, 144)]
        to_sp(own, own, fin_ss.at[j], fin_rs.at[j], j).wait_recv()
        to_sp(rest, rest, rest_ss.at[j], rest_rs.at[j], j).wait_recv()
        pass_on(j).start()
        put_fin(j).start()
    loop(1, NSP // 2, relay)
    loop(1, NSP // 2, lambda u: send_rest(u).wait_send())

    def recv_core(u):
        j = lax.rem(sibling + NSP - 2 * u, NSP)
        to_sp(fin.at[j], fin.at[j], core_ss.at[j], core_rs.at[j], sibling).wait_recv()
        put_fin(j).start()
    loop(0, NSP // 2, recv_core)

    loop(1, NSP // 2, lambda u: pass_on(lax.rem(me + NSP - 2 * u, NSP)).wait_send())
    pass_on(me).wait_send()
    put_upd.wait()
    loop(0, NSP, lambda j: put_fin(j).wait())


def outputs(fin_hbm, upd_hbm, upd_out, grad_out, fin, upd, grad, sem):
    xi = lax.rem(lax.axis_index("dp"), 4)
    take = pltpu.make_async_copy(upd_hbm, upd, sem.at[HEADS // 2])
    move = pltpu.make_async_copy(upd, upd_out, sem.at[HEADS // 2])

    def get(j):
        return pltpu.make_async_copy(fin_hbm.at[pl.ds(j, 2)], fin.at[pl.ds(j, 2)],
                                     sem.at[HEADS // 2 + 1 + j // 2])
    for j in range(0, HEADS, 2):
        get(j).start()
    take.start()
    turn = [lax.rem(k + 4 - xi, 4) for k in range(4)]
    start = [pl.multiple_of(lax.select(r == 0, 0, 16 + 48 * r), 16) for r in turn]

    def head_rows(j):
        tiles = [fin[j, pl.ds(start[i // 3] + 16 * (i % 3), 16)].astype(f32) for i in range(12)]
        spare = fin[j, 48:64].astype(f32)
        low = [tiles[10][:8], tiles[10][8:], tiles[11][:8], tiles[11][8:], spare[:8]]
        return [jnp.concatenate(row, axis=1) for row in (tiles[:5], tiles[5:10], low)]
    for j in range(0, HEADS, 2):
        get(j).wait()
        two = jnp.concatenate(head_rows(j) + head_rows(j + 1), axis=0)
        here = slice(HD * j, HD * j + 2 * HD)
        grad[here] = two
        pltpu.make_async_copy(grad.at[here], grad_out.at[here], sem.at[j // 2]).start()
    take.wait()
    move.start()
    for j in range(0, HEADS, 2):
        here = slice(HD * j, HD * j + 2 * HD)
        pltpu.make_async_copy(grad.at[here], grad_out.at[here], sem.at[j // 2]).wait()
    move.wait()


def on_device(features, timestep, group_gain, conv_weight, time_weight, norm_gain, qkv_weight,
              out_weight, cotangent):
    vmem = pl.BlockSpec(memory_space=pltpu.VMEM)
    hbm = pl.BlockSpec(memory_space=pl.ANY)
    dma = pltpu.SemaphoreType.DMA
    updated, tiles = pl.pallas_call(
        kernel,
        out_shape=(
            jax.ShapeDtypeStruct((T, C), bf16),
            jax.ShapeDtypeStruct((NSP, 13 * 16, L), bf16),
        ),
        in_specs=[vmem, vmem, vmem] + [hbm] * 6,
        out_specs=(hbm, hbm),
        scratch_shapes=[
            pltpu.VMEM((4 * W, C), bf16),
            pltpu.VMEM((3, 3 * C, C), bf16),
            pltpu.VMEM((TEMB, C), bf16),
            pltpu.VMEM((C, 3 * C), bf16),
            pltpu.VMEM((C, C), bf16),
            pltpu.VMEM((2, T, C), bf16),
            pltpu.VMEM((HEADS // 2, C, 2 * L), bf16),
            pltpu.VMEM((2, HEADS // 2 * HP, C), bf16),
            pltpu.VMEM((4 * W, 3 * C), bf16),
            pltpu.VMEM((T, C), bf16),
            pltpu.VMEM((NSP, 8, L), f32),
            pltpu.VMEM((NSP, T, L), bf16),
            pltpu.VMEM((NSP, T, L), bf16),
            pltpu.VMEM((2, T, NSP * T), f32),
            pltpu.VMEM((T, L), f32),
            pltpu.VMEM((NSP // 2, HP, 2 * T), bf16),
            pltpu.VMEM((NSP // 2, HP, 2 * T), bf16),
            pltpu.VMEM((NSP // 2, 4, 64, L), bf16),
            pltpu.VMEM((4, NSP // 2, 64, L), bf16),
            pltpu.VMEM((2, T, C), f32),
            pltpu.VMEM((T, C), f32),
            pltpu.VMEM((4, 64, L), bf16),
            pltpu.VMEM((NSP, 13 * 16, L), bf16),
            pltpu.VMEM((8, T, L), f32),
            pltpu.VMEM((8, T, L), f32),
            dma((6,)), dma((16,)), dma((16,)), dma((2,)), dma((2,)), dma((16,)), dma((16,)),
            dma((8,)), dma((8,)), dma((8, 4)), dma((4, 8)),
            dma((1,)), dma((1,)), dma((1,)), dma((1,)),
            dma((4,)), dma((4,)), dma((4,)), dma((4,)),
            dma((16,)), dma((16,)), dma((16,)), dma((16,)), dma((16,)), dma((16,)), dma((16,)),
        ],
        compiler_params=pltpu.CompilerParams(
            collective_id=0, has_side_effects=True, vmem_limit_bytes=60 * 2**20),
        name="level",
    )(
        timestep, group_gain, norm_gain, features.reshape(T, C),
        conv_weight.reshape(3, 3 * C, C), time_weight, qkv_weight, out_weight,
        cotangent.reshape(T, C),
    )
    updated, out_grad = pl.pallas_call(
        outputs,
        out_shape=(
            jax.ShapeDtypeStruct((T, C), bf16),
            jax.ShapeDtypeStruct((C, C), f32),
        ),
        in_specs=[hbm, hbm],
        out_specs=(hbm, hbm),
        scratch_shapes=[
            pltpu.VMEM((NSP, 13 * 16, L), bf16),
            pltpu.VMEM((T, C), bf16),
            pltpu.VMEM((C, C), f32),
            dma((HEADS + 1,)),
        ],
        compiler_params=pltpu.CompilerParams(vmem_limit_bytes=63 * 2**20),
        name="outputs",
    )(tiles, updated)
    return updated.reshape(1, ROWS, W, C), out_grad


def solution(mesh):
    slab = P("dp", "sp", None, None)
    return jax.shard_map(
        on_device, mesh=mesh,
        in_specs=(slab, P("dp"), P(), P(), P(), P(), P(), P(), slab),
        out_specs=(slab, P()), check_vma=False,
    )
```
